256 devices in a mesh: dp: 8 (over x, core), shard: 32 (over y, z).
Axes of the slice: x: 4, y: 4, z: 8, core: 2. Of those that a mesh axis runs over, the one named last changes fastest.
Arguments:
- grads: bfloat16 [8, 256, 512, 512], P('dp', None, 'shard'), may hold values from -120 to 120
- owned: int32 [8, 32], replicated, may hold values from 0 to 31, as said below
- left_stat: float32 [8, 32, 512, 512], P('dp', 'shard'), may hold values from -1 to 16, as said below
- right_stat: float32 [8, 32, 512, 512], P('dp', 'shard'), may hold values from -1 to 16, as said below
Outputs:
- update: float32 [256, 512, 512], P('dp', 'shard')
- left_new: float32 [8, 32, 512, 512], P('dp', 'shard')
- right_new: float32 [8, 32, 512, 512], P('dp', 'shard')
The draws below stay inside these ranges and needn't reach their ends.
Inputs may be any that keep to these rules, and one draw needn't show every extreme that they name: `owned`: each row is a permutation of 0 to 31. `left_stat`: symmetric with a positive diagonal larger than the sum of its row's other magnitudes. `right_stat`: symmetric with a positive diagonal larger than the sum of its row's other magnitudes.
All inputs are finite; a program needn't handle non-finite values.
Results may differ from the reference program's by a relative error of at most 0.0003.
Values may be sent and summed in bfloat16 or wider, within the bound.
No kernel may reach another device: no remote copies, remote signals or barrier semaphores. Data moves between devices by JAX's collectives and lax.ppermute only.
A program may use at most 64 MiB of HBM per device.

```python
import math
import jax
import jax.numpy as jnp
from jax import lax

B = 512
NEWTON = 2
NBLK = 256
N_DP = 8
N_SHARD = 32


def draw_grads(key, part):
    key = jax.random.fold_in(key, 11)
    first = jax.random.fold_in(key, 0)
    shape = (N_DP, NBLK, B, B)
    place = jnp.arange(NBLK, dtype=jnp.float32) / max(NBLK - 1, 1)
    rising = 3.0 ** place
    values = jax.random.truncated_normal(first, -4.0, 4.0, shape, jnp.float32) * rising[None, :, None, None]
    return values.astype(jnp.bfloat16)


def draw_owned(key, part):
    key = jax.random.fold_in(key, 23)
    keys = jax.random.split(key, N_DP)
    return jax.vmap(lambda single: jax.random.permutation(single, N_SHARD))(keys).astype(jnp.int32)


def symmetric_stat(key, highest):
    first, second = jax.random.split(key)
    noise = jax.random.uniform(first, (N_DP, N_SHARD, B, B), jnp.float32, -1.0, 1.0)
    spread = (noise + jnp.swapaxes(noise, -1, -2)) * (0.5 / B)
    diagonal = jnp.exp(jax.random.uniform(second, (N_DP, N_SHARD, B), jnp.float32, math.log(2.0), math.log(highest)))
    eye = jnp.eye(B, dtype=jnp.float32)
    return spread * (1.0 - eye) + diagonal[..., None] * eye


def draw_left_stat(key, part):
    key = jax.random.fold_in(key, 31)
    return symmetric_stat(key, 8.0)


def draw_right_stat(key, part):
    key = jax.random.fold_in(key, 37)
    return symmetric_stat(key, 8.0)


def setup_inputs(seed: int = 0) -> dict:
    splits = jax.random.split(jax.random.key(seed), 5)
    return {
        "grads": draw_grads(jax.random.fold_in(splits[4], 71), 0),
        "owned": draw_owned(jax.random.fold_in(splits[4], 71), 0),
        "left_stat": draw_left_stat(jax.random.fold_in(splits[4], 71), 0),
        "right_stat": draw_right_stat(jax.random.fold_in(splits[4], 71), 0),
    }


def product(left, right):
    return jnp.dot(left, right, precision=lax.Precision.HIGHEST, preferred_element_type=jnp.float32)

def inverse_root(stat):
    eye = jnp.eye(stat.shape[0], dtype=jnp.float32)
    shifted = stat + 1e-06 * eye
    norm_value = jnp.sqrt(jnp.sum(shifted * shifted))
    matrix = shifted / norm_value
    root = eye * norm_value ** (-0.25)
    for step in range(NEWTON):
        factor = (5.0 * eye - matrix) * 0.25
        root = product(root, factor)
        square = product(factor, factor)
        matrix = product(product(square, square), matrix)
    return root

def precondition(grad, left_old, right_old):
    order = grad.shape[0]
    left_fresh = 0.95 * left_old + product(grad, grad.T) / order
    right_fresh = 0.95 * right_old + product(grad.T, grad) / order
    shaped = product(product(inverse_root(left_fresh), grad), inverse_root(right_fresh))
    graft = jnp.sqrt(jnp.mean(grad * grad) + 1e-06) / jnp.sqrt(jnp.mean(shaped * shaped) + 1e-06)
    return (left_fresh, right_fresh, shaped * graft)

def reference(grads, owned, left_stat, right_stat):
    summed = lax.optimization_barrier(jnp.sum(grads, axis=0, dtype=jnp.float32))
    index = (jnp.arange(N_DP, dtype=jnp.int32)[:, None] * N_SHARD + owned).reshape(-1).astype(jnp.int32)
    picked = jnp.take(summed, index, axis=0)

    def single(items):
        return precondition(items[0], items[1], items[2])
    left_fresh, right_fresh, shaped = lax.map(single, (picked, left_stat.reshape(-1, B, B), right_stat.reshape(-1, B, B)))
    layer = 1.0 / jnp.sqrt(jnp.sum(summed * summed) / (NBLK * B * B) + 1e-06)
    scaled = shaped * layer
    update = jnp.zeros((NBLK, B, B), jnp.float32).at[index].set(scaled)
    return (update, left_fresh.reshape(N_DP, N_SHARD, B, B), right_fresh.reshape(N_DP, N_SHARD, B, B))
```

```python
import jax
import jax.numpy as jnp
from jax import lax
from jax.experimental import pallas as pl
from jax.experimental.pallas import tpu as pltpu
from jax.sharding import PartitionSpec as P

LIMIT = 32700.0
STEPS = 128.0
K = 1.25**6
EPS = 1e-06
f32, bf16 = jnp.float32, jnp.bfloat16
VMEM = pl.BlockSpec(memory_space=pltpu.VMEM)
SMEM = pl.BlockSpec(memory_space=pltpu.SMEM)


def params(**more):
    return pltpu.CompilerParams(vmem_limit_bytes=48 << 20, **more)


def encode(strip):
    columns = [strip[:, c : c + 128] for c in range(0, strip.shape[1], 128)]
    top = columns[0]
    top = jnp.abs(top)
    for column in columns[1:]:
        top = jnp.maximum(top, jnp.abs(column))
    top = jnp.maximum(jnp.maximum(top[:8], top[8:]), 1e-30)
    code = jnp.ceil(jnp.log2(top) * STEPS)
    gain = jnp.exp2(code * (-1.0 / STEPS)) * LIMIT
    gain = jnp.concatenate([gain, gain], axis=0)
    coded = [jnp.round(column * gain).astype(jnp.int32) for column in columns]
    return coded, code.astype(jnp.int32)


def decode_gain(code):
    gain = jnp.exp2(code * (1.0 / STEPS)) * (1.0 / LIMIT)
    return jnp.concatenate([gain, gain], axis=0)


def encode_number(number):
    power = jnp.ceil(jnp.log2(jnp.maximum(number, 1e-30))) + 1.0
    digits = number * jnp.exp2(-power) * 16384.0
    high = jnp.floor(digits)
    low = jnp.floor((digits - high) * 16384.0)
    row = lax.broadcasted_iota(jnp.int32, number.shape, 0)
    return jnp.where(row == 0, power, jnp.where(row == 1, high, low)).astype(jnp.int32)


def decode_numbers(rows):
    power, high, low = rows[:, 0:1], rows[:, 1:2], rows[:, 2:3]
    return jnp.sum((high + low * (1.0 / 16384.0)) * (1.0 / 16384.0) * jnp.exp2(power), axis=0)


def split(matrix):
    high = matrix.astype(bf16)
    return high, (matrix - high.astype(f32)).astype(bf16)


def dot3(left, right, dims=((1,), (0,))):
    dims = (dims, ((), ()))
    lh, ll = left
    rh, rl = right
    out = lax.dot_general(lh, rl, dims, preferred_element_type=f32)
    out += lax.dot_general(ll, rh, dims, preferred_element_type=f32)
    return out + lax.dot_general(lh, rh, dims, preferred_element_type=f32)


def eye_like(matrix):
    row = lax.broadcasted_iota(jnp.int32, matrix.shape, 0)
    column = lax.broadcasted_iota(jnp.int32, matrix.shape, 1)
    return row == column


def inverse_root(stat):
    diagonal = eye_like(stat)
    shifted = stat + jnp.where(diagonal, EPS, 0.0)
    norm = jnp.sqrt(jnp.sum(shifted * shifted, keepdims=True))
    u = shifted * (0.2 / norm)
    us = split(u)
    u2 = dot3(us, us)
    u3 = dot3(split(u2), us)
    inner = jnp.where(diagonal, -10.0 * K, 0.0) + 10.0 * K * u - 5.0 * K * u2 + K * u3
    outer = jnp.where(diagonal, 1.5625, 0.0) - (1.5625 + K) * u + 5.0 * K * u2
    root = outer + dot3(split(u3), split(inner))
    return root * lax.rsqrt(jnp.sqrt(norm))


def invert(order_ref, slot_ref):
    def step(j, _):
        slot_ref[order_ref[j]] = j
        return 0

    lax.fori_loop(0, order_ref.shape[0], step, 0)


def sum_kernel(order_ref, parts_ref, out_ref, slot_ref, code_ref, square_ref):
    step, steps = pl.program_id(0), pl.num_programs(0)
    count = parts_ref.shape[1]

    @pl.when(step == 0)
    def _():
        invert(order_ref, slot_ref)
        square_ref[...] = jnp.zeros_like(square_ref)

    for b in range(count):
        strip = parts_ref[0, b].astype(f32)
        for i in range(1, parts_ref.shape[0]):
            strip += parts_ref[i, b].astype(f32)
        square = strip * strip
        for c in range(0, strip.shape[1], 128):
            square_ref[...] += square[:8, c : c + 128] + square[8:, c : c + 128]
        slot = slot_ref[step * count + b]
        coded, code = encode(strip)
        for c, column in enumerate(coded):
            out_ref[slot, 16 * c : 16 * c + 16, :] = column.astype(jnp.int16)
        code_ref[slot] = code

    @pl.when(step == steps - 1)
    def _():
        whole = jnp.broadcast_to(jnp.sum(square_ref[...], keepdims=True), square_ref.shape)
        number = encode_number(whole)
        for j in range(out_ref.shape[0]):
            tail = jnp.concatenate([code_ref[j], number], axis=0)
            out_ref[j, 64:80, :] = tail.astype(jnp.int16)


def left_kernel(coded_ref, stat_ref, high_ref, low_ref, stat_out, root_out, sums_ref, grad_ref):
    shards = coded_ref.shape[0]
    square = jnp.zeros((16, 128), f32)
    for j in range(shards):
        tail = coded_ref[j, 64:80, :].astype(jnp.int32).astype(f32)
        gain = decode_gain(tail[:8])
        for c in range(4):
            piece = coded_ref[j, 16 * c : 16 * c + 16, :].astype(jnp.int32).astype(f32) * gain
            square += piece * piece
            grad_ref[16 * j : 16 * j + 16, 128 * c : 128 * c + 128] = piece
    tails = jnp.stack([coded_ref[j, 64:80, :].astype(jnp.int32).astype(f32)[8:] for j in range(shards)])
    sums_ref[0:8] = jnp.broadcast_to(decode_numbers(tails), (8, 128))
    sums_ref[8:16] = jnp.broadcast_to(jnp.sum(square, keepdims=True), (8, 128))
    pair = split(grad_ref[...])
    high_ref[...], low_ref[...] = pair
    fresh = 0.95 * stat_ref[...] + dot3(pair, pair, ((1,), (1,))) * (1.0 / grad_ref.shape[0])
    stat_out[...] = fresh
    root_out[...] = inverse_root(fresh)


def right_kernel(high_ref, low_ref, stat_ref, stat_out, root_out):
    pair = (high_ref[...], low_ref[...])
    fresh = 0.95 * stat_ref[...] + dot3(pair, pair, ((0,), (0,))) * (1.0 / stat_ref.shape[0])
    stat_out[...] = fresh
    root_out[...] = inverse_root(fresh)


def shape_kernel(high_ref, low_ref, left_ref, right_ref, sums_ref, total_ref, out_ref, shaped_ref):
    order = high_ref.shape[0]
    half = dot3(split(left_ref[...]), (high_ref[...], low_ref[...]))
    shaped = dot3(split(half), split(right_ref[...]))
    cells = 1.0 / (order * order)
    mean = jnp.sum(shaped * shaped, keepdims=True) * cells
    graft = jnp.sqrt(sums_ref[8:9, 0:1] * cells + EPS) / jnp.sqrt(mean + EPS)
    shaped_ref[...] = shaped * graft
    number = encode_number(total_ref[...])
    for j in range(out_ref.shape[0]):
        coded, code = encode(shaped_ref[16 * j : 16 * j + 16, :])
        for c, column in enumerate(coded):
            out_ref[j, 16 * c : 16 * c + 16, :] = column.astype(jnp.int16)
        out_ref[j, 64:80, :] = jnp.concatenate([code, number], axis=0).astype(jnp.int16)


def update_kernel(groups, cells, order_ref, coded_ref, out_ref):
    tails = jnp.stack([coded_ref[j, 64:80, :].astype(jnp.int32).astype(f32)[8:] for j in range(groups)])
    layer = 1.0 / jnp.sqrt(decode_numbers(tails) * (1.0 / cells) + EPS)
    for j in range(coded_ref.shape[0]):
        slot = order_ref[j]
        tail = coded_ref[j, 64:80, :].astype(jnp.int32).astype(f32)
        gain = decode_gain(tail[:8]) * layer
        for c in range(4):
            piece = coded_ref[j, 16 * c : 16 * c + 16, :].astype(jnp.int32).astype(f32) * gain
            out_ref[slot, :, 128 * c : 128 * c + 128] = piece


def body(grads, owned, left_stat, right_stat):
    shards, groups = lax.axis_size("shard"), lax.axis_size("dp")
    group = lax.axis_index("dp")
    blocks, strip, width = grads.shape[1:]
    mine = lax.dynamic_index_in_dim(owned, group, 0, keepdims=False)
    square = jax.ShapeDtypeStruct((width, width), f32)
    halves = jax.ShapeDtypeStruct((width, width), bf16)
    wire = jax.ShapeDtypeStruct((shards, 80, 128), jnp.int16)

    parts = lax.all_to_all(grads[0], "dp", split_axis=0, concat_axis=0, tiled=True)
    parts = parts.reshape(groups, shards, strip, width)
    chunk = 8
    strips = pl.pallas_call(
        sum_kernel,
        grid=(shards // chunk,),
        in_specs=[SMEM, pl.BlockSpec((groups, chunk, strip, width), lambda i: (0, i, 0, 0))],
        out_specs=pl.BlockSpec((shards, 80, 128), lambda i: (0, 0, 0)),
        out_shape=wire,
        scratch_shapes=[
            pltpu.SMEM((shards,), jnp.int32),
            pltpu.VMEM((shards, 8, 128), jnp.int32),
            pltpu.VMEM((8, 128), f32),
        ],
        compiler_params=params(),
        name="sum_strips",
    )(mine, parts)
    strips = lax.all_to_all(strips, "shard", split_axis=0, concat_axis=0, tiled=True)
    high, low, left_fresh, left_root, sums = pl.pallas_call(
        left_kernel,
        in_specs=[VMEM, VMEM],
        out_specs=[VMEM] * 5,
        out_shape=[halves, halves, square, square, jax.ShapeDtypeStruct((16, 128), f32)],
        scratch_shapes=[pltpu.VMEM((width, width), f32)],
        compiler_params=params(),
        name="left",
    )(strips, left_stat[0, 0])
    pairs = [
        (((d + s) % groups) * shards + s, d * shards + s) for d in range(groups) for s in range(shards)
    ]
    total = lax.ppermute(sums[:8], ("dp", "shard"), pairs)
    right_fresh, right_root = pl.pallas_call(
        right_kernel,
        in_specs=[VMEM] * 3,
        out_specs=[VMEM] * 2,
        out_shape=[square, square],
        compiler_params=params(),
        cost_estimate=pl.CostEstimate(flops=10 * 2 * width**3, bytes_accessed=5 << 20, transcendentals=0),
        name="right",
    )(high, low, right_stat[0, 0])
    pieces = pl.pallas_call(
        shape_kernel,
        in_specs=[VMEM] * 6,
        out_specs=VMEM,
        out_shape=wire,
        scratch_shapes=[pltpu.VMEM((width, width), f32)],
        compiler_params=params(),
        name="shape",
    )(high, low, left_root, right_root, sums, total)
    pieces = lax.all_to_all(pieces, "shard", split_axis=0, concat_axis=0, tiled=True)
    update = pl.pallas_call(
        lambda *refs: update_kernel(groups, blocks * width * width, *refs),
        in_specs=[SMEM, VMEM],
        out_specs=VMEM,
        out_shape=jax.ShapeDtypeStruct((shards, strip, width), f32),
        compiler_params=params(),
        name="update",
    )(mine, pieces)
    return update, left_fresh[None, None], right_fresh[None, None]


def solution(mesh):
    return jax.shard_map(
        body,
        mesh=mesh,
        in_specs=(
            P("dp", None, "shard", None),
            P(),
            P("dp", "shard", None, None),
            P("dp", "shard", None, None),
        ),
        out_specs=(
            P("dp", "shard", None),
            P("dp", "shard", None, None),
            P("dp", "shard", None, None),
        ),
        check_vma=False,
    )
```

```python
import jax
import jax.numpy as jnp
from jax import lax
from jax.experimental import pallas as pl
from jax.experimental.pallas import tpu as pltpu
from jax.sharding import PartitionSpec as P

ROWS = 72
LIMIT = 32700.0
STEPS = 128.0
K = 1.25**6
EPS = 1e-06
f32, bf16 = jnp.float32, jnp.bfloat16
VMEM = pl.BlockSpec(memory_space=pltpu.VMEM)
SMEM = pl.BlockSpec(memory_space=pltpu.SMEM)


def params(**more):
    return pltpu.CompilerParams(vmem_limit_bytes=48 << 20, **more)


def upper_rows():
    return lax.broadcasted_iota(jnp.int32, (8, 128), 0) < 4


def encode(strip, number=None):
    columns = [strip[:, c : c + 128] for c in range(0, strip.shape[1], 128)]
    top = jnp.abs(columns[0])
    for column in columns[1:]:
        top = jnp.maximum(top, jnp.abs(column))
    top = jnp.maximum(top[:8], top[8:])
    top = jnp.maximum(jnp.maximum(top, pltpu.roll(top, 4, 0)), 1e-30)
    code = jnp.ceil(jnp.log2(top) * STEPS)
    gain = jnp.exp2(code * (-1.0 / STEPS)) * LIMIT
    gain = jnp.concatenate([gain, gain], axis=0)
    coded = [jnp.round(column * gain) for column in columns]
    tail = code if number is None else jnp.where(upper_rows(), code, number)
    return jnp.concatenate(coded + [tail], axis=0).astype(jnp.int32)


def decode_gain(tail):
    code = jnp.where(upper_rows(), tail, pltpu.roll(tail, 4, 0))
    gain = jnp.exp2(code * (1.0 / STEPS)) * (1.0 / LIMIT)
    return jnp.concatenate([gain, gain], axis=0)


def decode(coded, factor=None):
    gain = decode_gain(coded[64:])
    if factor is not None:
        gain = gain * factor
    return [coded[r : r + 16] * gain for r in range(0, 64, 16)]


def load(ref, pair):
    both = ref[2 * ROWS * pair : 2 * ROWS * (pair + 1), :].astype(jnp.int32).astype(f32)
    return both[:ROWS], both[ROWS:]


def store(ref, pair, first, second):
    both = jnp.concatenate([first, second], axis=0)
    ref[2 * ROWS * pair : 2 * ROWS * (pair + 1), :] = both.astype(jnp.int16)


def encode_number(number):
    power = jnp.ceil(jnp.log2(jnp.maximum(number, 1e-30))) + 1.0
    digits = number * jnp.exp2(-power) * 16384.0
    high = jnp.floor(digits)
    low = jnp.floor((digits - high) * 16384.0)
    row = lax.broadcasted_iota(jnp.int32, number.shape, 0)
    return jnp.where(row == 4, power, jnp.where(row == 5, high, low))


def decode_number(tail):
    power, high, low = tail[4:5], tail[5:6], tail[6:7]
    return (high + low * (1.0 / 16384.0)) * (1.0 / 16384.0) * jnp.exp2(power)


def split(matrix):
    high = matrix.astype(bf16)
    return high, (matrix - high.astype(f32)).astype(bf16)


def dot3(left, right, dims=((1,), (0,))):
    dims = (dims, ((), ()))
    lh, ll = left
    rh, rl = right
    out = lax.dot_general(lh, rl, dims, preferred_element_type=f32)
    out += lax.dot_general(ll, rh, dims, preferred_element_type=f32)
    return out + lax.dot_general(lh, rh, dims, preferred_element_type=f32)


def eye_like(matrix):
    row = lax.broadcasted_iota(jnp.int32, matrix.shape, 0)
    column = lax.broadcasted_iota(jnp.int32, matrix.shape, 1)
    return row == column


def inverse_root(stat):
    diagonal = eye_like(stat)
    shifted = stat + jnp.where(diagonal, EPS, 0.0)
    norm = jnp.sqrt(jnp.sum(shifted * shifted, keepdims=True))
    u = shifted * (0.2 / norm)
    us = split(u)
    u2 = dot3(us, us)
    u3 = dot3(split(u2), us)
    inner = jnp.where(diagonal, -10.0 * K, 0.0) + 10.0 * K * u - 5.0 * K * u2 + K * u3
    outer = jnp.where(diagonal, 1.5625, 0.0) - (1.5625 + K) * u + 5.0 * K * u2
    root = outer + dot3(split(u3), split(inner))
    return root * lax.rsqrt(jnp.sqrt(norm))


def invert(order_ref, slot_ref):
    def step(j, _):
        slot_ref[order_ref[j]] = j
        return 0

    lax.fori_loop(0, order_ref.shape[0], step, 0)


def pair_kernel(pick_ref, own_ref, other_ref, out_ref):
    for p in range(other_ref.shape[0] // 2):
        coded = [encode(own_ref[0, b].astype(f32) + other_ref[b].astype(f32)) for b in (2 * p, 2 * p + 1)]
        store(out_ref, p, *coded)


def sum_kernel(pick_ref, order_ref, own_ref, other_ref, *refs):
    part_refs, (out_ref, slot_ref, coded_ref, square_ref) = refs[:-4], refs[-4:]
    step, steps = pl.program_id(0), pl.num_programs(0)
    count = other_ref.shape[0]

    @pl.when(step == 0)
    def _():
        invert(order_ref, slot_ref)
        square_ref[...] = jnp.zeros_like(square_ref)

    total = jnp.zeros((8, 128), f32)
    for p in range(count // 2):
        parts = [load(ref, p) for ref in part_refs]
        for i in range(2):
            b = 2 * p + i
            strip = own_ref[0, b].astype(f32) + other_ref[b].astype(f32)
            pieces = [decode(part[i]) for part in parts]
            columns = [
                strip[:, 128 * c : 128 * c + 128] + sum(piece[c] for piece in pieces[1:]) + pieces[0][c]
                for c in range(4)
            ]
            for column in columns:
                square = column * column
                total += square[:8] + square[8:]
            coded_ref[slot_ref[step * count + b]] = encode(jnp.concatenate(columns, axis=1))
    square_ref[...] += total

    @pl.when(step == steps - 1)
    def _():
        whole = jnp.broadcast_to(jnp.sum(square_ref[...], keepdims=True), square_ref.shape)
        number = encode_number(whole).astype(jnp.int32)
        for p in range(coded_ref.shape[0] // 2):
            both = []
            for j in (2 * p, 2 * p + 1):
                tail = jnp.where(upper_rows(), coded_ref[j, 64:72, :], number)
                both.append(jnp.concatenate([coded_ref[j, 0:64, :], tail], axis=0))
            store(out_ref, p, *both)


def left_kernel(coded_ref, stat_ref, high_ref, low_ref, stat_out, root_out, sums_ref, grad_ref):
    square = jnp.zeros((16, 128), f32)
    group = jnp.zeros((1, 128), f32)
    for p in range(coded_ref.shape[0] // (2 * ROWS)):
        for i, coded in enumerate(load(coded_ref, p)):
            row = 16 * (2 * p + i)
            group += decode_number(coded[64:])
            for c, piece in enumerate(decode(coded)):
                square += piece * piece
                grad_ref[row : row + 16, 128 * c : 128 * c + 128] = piece
    sums_ref[0:8] = jnp.broadcast_to(group, (8, 128))
    sums_ref[8:16] = jnp.broadcast_to(jnp.sum(square, keepdims=True), (8, 128))
    pair = split(grad_ref[...])
    high_ref[...], low_ref[...] = pair
    fresh = 0.95 * stat_ref[...] + dot3(pair, pair, ((1,), (1,))) * (1.0 / grad_ref.shape[0])
    stat_out[...] = fresh
    root_out[...] = inverse_root(fresh)


def right_kernel(high_ref, low_ref, stat_ref, stat_out, root_out):
    pair = (high_ref[...], low_ref[...])
    fresh = 0.95 * stat_ref[...] + dot3(pair, pair, ((0,), (0,))) * (1.0 / stat_ref.shape[0])
    stat_out[...] = fresh
    root_out[...] = inverse_root(fresh)


def shape_kernel(high_ref, low_ref, left_ref, right_ref, sums_ref, total_ref, out_ref, shaped_ref):
    order = high_ref.shape[0]
    half = dot3(split(left_ref[...]), (high_ref[...], low_ref[...]))
    shaped = dot3(split(half), split(right_ref[...]))
    cells = 1.0 / (order * order)
    mean = jnp.sum(shaped * shaped, keepdims=True) * cells
    graft = jnp.sqrt(sums_ref[8:9, 0:1] * cells + EPS) / jnp.sqrt(mean + EPS)
    shaped_ref[...] = shaped * graft
    number = encode_number(total_ref[...])
    for p in range(order // 32):
        rows = 32 * p
        store(
            out_ref,
            p,
            encode(shaped_ref[rows : rows + 16, :], number),
            encode(shaped_ref[rows + 16 : rows + 32, :], number),
        )


def update_kernel(groups, cells, order_ref, coded_ref, out_ref):
    total = jnp.zeros((1, 128), f32)
    for p in range(groups // 2):
        for coded in load(coded_ref, p):
            total += decode_number(coded[64:])
    layer = 1.0 / jnp.sqrt(total * (1.0 / cells) + EPS)
    for p in range(out_ref.shape[0] // 2):
        for i, coded in enumerate(load(coded_ref, p)):
            slot = order_ref[2 * p + i]
            for c, piece in enumerate(decode(coded, layer)):
                out_ref[slot, :, 128 * c : 128 * c + 128] = piece


def body(grads, owned, left_stat, right_stat):
    shards, groups = lax.axis_size("shard"), lax.axis_size("dp")
    group = lax.axis_index("dp")
    blocks, strip, width = grads.shape[1:]
    core, chip, chips = group % 2, group // 2, groups // 2
    mine = lax.dynamic_index_in_dim(owned, group, 0, keepdims=False)
    square = jax.ShapeDtypeStruct((width, width), f32)
    halves = jax.ShapeDtypeStruct((width, width), bf16)
    wire = jax.ShapeDtypeStruct((shards * ROWS, 128), jnp.int16)
    grouped = grads[0].reshape(groups, shards, strip, width)
    swap = [(d, d ^ 1) for d in range(groups)]
    chunk = 8
    own_block = pl.BlockSpec((1, chunk, strip, width), lambda i, pick, *_: (pick[0], i, 0, 0))
    other_block = pl.BlockSpec((chunk, strip, width), lambda i, *_: (i, 0, 0))
    wire_block = pl.BlockSpec((chunk * ROWS, 128), lambda i, *_: (i, 0))

    received = []
    for ahead in (2, 1, 3, 0):
        target = 2 * ((chip + ahead) % chips)
        other = lax.dynamic_index_in_dim(grouped, target + 1 - core, 0, keepdims=False)
        other = lax.ppermute(other, "dp", swap)
        pick = (target + core).reshape(1)
        if ahead == 0:
            break
        sums = pl.pallas_call(
            pair_kernel,
            grid_spec=pltpu.PrefetchScalarGridSpec(
                num_scalar_prefetch=1,
                grid=(shards // chunk,),
                in_specs=[own_block, other_block],
                out_specs=wire_block,
            ),
            out_shape=wire,
            compiler_params=params(),
            name=f"pair_{ahead}",
        )(pick, grouped, other)
        along = [(d, (d + 2 * ahead) % groups) for d in range(groups)]
        received.append(lax.ppermute(sums, "dp", along))
    strips = pl.pallas_call(
        sum_kernel,
        grid_spec=pltpu.PrefetchScalarGridSpec(
            num_scalar_prefetch=2,
            grid=(shards // chunk,),
            in_specs=[own_block, other_block] + [wire_block] * len(received),
            out_specs=pl.BlockSpec((shards * ROWS, 128), lambda i, *_: (0, 0)),
            scratch_shapes=[
                pltpu.SMEM((shards,), jnp.int32),
                pltpu.VMEM((shards, ROWS, 128), jnp.int32),
                pltpu.VMEM((8, 128), f32),
            ],
        ),
        out_shape=wire,
        compiler_params=params(),
        name="sum_strips",
    )(pick, mine, grouped, other, *received)
    strips = lax.all_to_all(strips, "shard", split_axis=0, concat_axis=0, tiled=True)
    high, low, left_fresh, left_root, sums = pl.pallas_call(
        left_kernel,
        in_specs=[VMEM, VMEM],
        out_specs=[VMEM] * 5,
        out_shape=[halves, halves, square, square, jax.ShapeDtypeStruct((16, 128), f32)],
        scratch_shapes=[pltpu.VMEM((width, width), f32)],
        compiler_params=params(),
        name="left",
    )(strips, left_stat[0, 0])
    pairs = [
        (((d + s) % groups) * shards + s, d * shards + s) for d in range(groups) for s in range(shards)
    ]
    total = lax.ppermute(sums[:8], ("dp", "shard"), pairs)
    right_fresh, right_root = pl.pallas_call(
        right_kernel,
        in_specs=[VMEM] * 3,
        out_specs=[VMEM] * 2,
        out_shape=[square, square],
        compiler_params=params(),
        cost_estimate=pl.CostEstimate(flops=10 * 2 * width**3, bytes_accessed=5 << 20, transcendentals=0),
        name="right",
    )(high, low, right_stat[0, 0])
    pieces = pl.pallas_call(
        shape_kernel,
        in_specs=[VMEM] * 6,
        out_specs=VMEM,
        out_shape=wire,
        scratch_shapes=[pltpu.VMEM((width, width), f32)],
        compiler_params=params(),
        name="shape",
    )(high, low, left_root, right_root, sums, total)
    pieces = lax.all_to_all(pieces, "shard", split_axis=0, concat_axis=0, tiled=True)
    update = pl.pallas_call(
        lambda *refs: update_kernel(groups, blocks * width * width, *refs),
        in_specs=[SMEM, VMEM],
        out_specs=VMEM,
        out_shape=jax.ShapeDtypeStruct((shards, strip, width), f32),
        compiler_params=params(),
        name="update",
    )(mine, pieces)
    return update, left_fresh[None, None], right_fresh[None, None]


def solution(mesh):
    return jax.shard_map(
        body,
        mesh=mesh,
        in_specs=(
            P("dp", None, "shard", None),
            P(),
            P("dp", "shard", None, None),
            P("dp", "shard", None, None),
        ),
        out_specs=(
            P("dp", "shard", None),
            P("dp", "shard", None, None),
            P("dp", "shard", None, None),
        ),
        check_vma=False,
    )
```

```python
import jax
import jax.numpy as jnp
from jax import lax
from jax.experimental import pallas as pl
from jax.experimental.pallas import tpu as pltpu
from jax.sharding import PartitionSpec as P

ROWS = 72
LIMIT = 32700.0
STEPS = 128.0
K = 1.25**6
EPS = 1e-06
f32, bf16 = jnp.float32, jnp.bfloat16
VMEM = pl.BlockSpec(memory_space=pltpu.VMEM)
SMEM = pl.BlockSpec(memory_space=pltpu.SMEM)


def params(limit=40 << 20):
    return pltpu.CompilerParams(vmem_limit_bytes=limit)


def upper_rows():
    return lax.broadcasted_iota(jnp.int32, (8, 128), 0) < 4


def encode(strip, number=None):
    columns = [strip[:, c : c + 128] for c in range(0, strip.shape[1], 128)]
    top = jnp.abs(columns[0])
    for column in columns[1:]:
        top = jnp.maximum(top, jnp.abs(column))
    top = jnp.maximum(top[:8], top[8:])
    top = jnp.maximum(jnp.maximum(top, pltpu.roll(top, 4, 0)), 1e-30)
    code = jnp.ceil(jnp.log2(top) * STEPS)
    gain = jnp.exp2(code * (-1.0 / STEPS)) * LIMIT
    gain = jnp.concatenate([gain, gain], axis=0)
    coded = [jnp.round(column * gain) for column in columns]
    tail = code if number is None else jnp.where(upper_rows(), code, number)
    return jnp.concatenate(coded + [tail], axis=0).astype(jnp.int32)


def decode_gain(tail):
    code = jnp.where(upper_rows(), tail, pltpu.roll(tail, 4, 0))
    gain = jnp.exp2(code * (1.0 / STEPS)) * (1.0 / LIMIT)
    return jnp.concatenate([gain, gain], axis=0)


def decode(coded, factor=None):
    gain = decode_gain(coded[64:])
    if factor is not None:
        gain = gain * factor
    return [coded[r : r + 16] * gain for r in range(0, 64, 16)]


def load(ref, pair):
    both = ref[2 * ROWS * pair : 2 * ROWS * (pair + 1), :].astype(jnp.int32).astype(f32)
    return both[:ROWS], both[ROWS:]


def store(ref, pair, first, second):
    both = jnp.concatenate([first, second], axis=0)
    ref[2 * ROWS * pair : 2 * ROWS * (pair + 1), :] = both.astype(jnp.int16)


def encode_number(number):
    power = jnp.ceil(jnp.log2(jnp.maximum(number, 1e-30))) + 1.0
    digits = number * jnp.exp2(-power) * 16384.0
    high = jnp.floor(digits)
    low = jnp.floor((digits - high) * 16384.0)
    row = lax.broadcasted_iota(jnp.int32, number.shape, 0)
    return jnp.where(row == 4, power, jnp.where(row == 5, high, low))


def decode_number(tail):
    power, high, low = tail[4:5], tail[5:6], tail[6:7]
    return (high + low * (1.0 / 16384.0)) * (1.0 / 16384.0) * jnp.exp2(power)


def split(matrix):
    high = matrix.astype(bf16)
    return high, (matrix - high.astype(f32)).astype(bf16)


def dot3(left, right, dims=((1,), (0,))):
    dims = (dims, ((), ()))
    lh, ll = left
    rh, rl = right
    out = lax.dot_general(lh, rl, dims, preferred_element_type=f32)
    out += lax.dot_general(ll, rh, dims, preferred_element_type=f32)
    return out + lax.dot_general(lh, rh, dims, preferred_element_type=f32)


def eye_like(matrix):
    row = lax.broadcasted_iota(jnp.int32, matrix.shape, 0)
    column = lax.broadcasted_iota(jnp.int32, matrix.shape, 1)
    return row == column


def inverse_root(stat):
    diagonal = eye_like(stat)
    shifted = stat + jnp.where(diagonal, EPS, 0.0)
    norm = jnp.sqrt(jnp.sum(shifted * shifted, keepdims=True))
    u = shifted * (0.2 / norm)
    us = split(u)
    u2 = dot3(us, us)
    u3 = dot3(split(u2), us)
    inner = jnp.where(diagonal, -10.0 * K, 0.0) + 10.0 * K * u - 5.0 * K * u2 + K * u3
    outer = jnp.where(diagonal, 1.5625, 0.0) - (1.5625 + K) * u + 5.0 * K * u2
    root = outer + dot3(split(u3), split(inner))
    return root * lax.rsqrt(jnp.sqrt(norm))


def invert(order_ref, slot_ref):
    def step(j, _):
        slot_ref[order_ref[j]] = j
        return 0

    lax.fori_loop(0, order_ref.shape[0], step, 0)


def pair_kernel(own_ref, other_ref, *refs):
    for p in range(other_ref.shape[0] // 2):
        part = load(refs[0], p) if len(refs) > 1 else None
        coded = []
        for i in range(2):
            strip = own_ref[2 * p + i].astype(f32) + other_ref[2 * p + i].astype(f32)
            if part is not None:
                strip += jnp.concatenate(decode(part[i]), axis=1)
            coded.append(encode(strip))
        store(refs[-1], p, *coded)


def sum_kernel(order_ref, own_ref, other_ref, *refs):
    part_refs, (out_ref, slot_ref, coded_ref, square_ref) = refs[:4], refs[4:]
    step, steps = pl.program_id(0), pl.num_programs(0)
    count = other_ref.shape[0]

    @pl.when(step == 0)
    def _():
        invert(order_ref, slot_ref)
        square_ref[...] = jnp.zeros_like(square_ref)

    def add(parts_of_half):
        total = jnp.zeros((8, 128), f32)
        for p in range(count // 2):
            parts = [load(ref, p) for ref in parts_of_half]
            for i in range(2):
                b = 2 * p + i
                strip = own_ref[b].astype(f32) + other_ref[b].astype(f32)
                first, second = [decode(part[i]) for part in parts]
                columns = [strip[:, 128 * c : 128 * c + 128] + (first[c] + second[c]) for c in range(4)]
                for column in columns:
                    square = column * column
                    total += square[:8] + square[8:]
                coded_ref[slot_ref[step * count + b]] = encode(jnp.concatenate(columns, axis=1))
        square_ref[...] += total

    pl.when(step < steps // 2)(lambda: add(part_refs[:2]))
    pl.when(step >= steps // 2)(lambda: add(part_refs[2:]))

    @pl.when(step == steps - 1)
    def _():
        whole = jnp.broadcast_to(jnp.sum(square_ref[...], keepdims=True), square_ref.shape)
        number = encode_number(whole).astype(jnp.int32)
        for p in range(coded_ref.shape[0] // 2):
            both = []
            for j in (2 * p, 2 * p + 1):
                tail = jnp.where(upper_rows(), coded_ref[j, 64:72, :], number)
                both.append(jnp.concatenate([coded_ref[j, 0:64, :], tail], axis=0))
            store(out_ref, p, *both)


def left_kernel(coded_ref, stat_ref, high_ref, low_ref, stat_out, root_out, sums_ref, grad_ref):
    square = jnp.zeros((16, 128), f32)
    group = jnp.zeros((1, 128), f32)
    for p in range(coded_ref.shape[0] // (2 * ROWS)):
        for i, coded in enumerate(load(coded_ref, p)):
            row = 16 * (2 * p + i)
            group += decode_number(coded[64:])
            for c, piece in enumerate(decode(coded)):
                square += piece * piece
                grad_ref[row : row + 16, 128 * c : 128 * c + 128] = piece
    sums_ref[0:8] = jnp.broadcast_to(group, (8, 128))
    sums_ref[8:16] = jnp.broadcast_to(jnp.sum(square, keepdims=True), (8, 128))
    pair = split(grad_ref[...])
    high_ref[...], low_ref[...] = pair
    fresh = 0.95 * stat_ref[...] + dot3(pair, pair, ((1,), (1,))) * (1.0 / grad_ref.shape[0])
    stat_out[...] = fresh
    root_out[...] = inverse_root(fresh)


def right_kernel(high_ref, low_ref, stat_ref, stat_out, root_out):
    pair = (high_ref[...], low_ref[...])
    fresh = 0.95 * stat_ref[...] + dot3(pair, pair, ((0,), (0,))) * (1.0 / stat_ref.shape[0])
    stat_out[...] = fresh
    root_out[...] = inverse_root(fresh)


def shape_kernel(high_ref, low_ref, left_ref, right_ref, sums_ref, total_ref, out_ref, shaped_ref):
    order = high_ref.shape[0]
    half = dot3(split(left_ref[...]), (high_ref[...], low_ref[...]))
    shaped = dot3(split(half), split(right_ref[...]))
    cells = 1.0 / (order * order)
    mean = jnp.sum(shaped * shaped, keepdims=True) * cells
    graft = jnp.sqrt(sums_ref[8:9, 0:1] * cells + EPS) / jnp.sqrt(mean + EPS)
    shaped_ref[...] = shaped * graft
    number = encode_number(total_ref[...])
    for p in range(order // 32):
        rows = 32 * p
        store(
            out_ref,
            p,
            encode(shaped_ref[rows : rows + 16, :], number),
            encode(shaped_ref[rows + 16 : rows + 32, :], number),
        )


def update_kernel(groups, cells, order_ref, coded_ref, out_ref):
    total = jnp.zeros((1, 128), f32)
    for p in range(groups // 2):
        for coded in load(coded_ref, p):
            total += decode_number(coded[64:])
    layer = 1.0 / jnp.sqrt(total * (1.0 / cells) + EPS)
    for p in range(out_ref.shape[0] // 2):
        for i, coded in enumerate(load(coded_ref, p)):
            slot = order_ref[2 * p + i]
            for c, piece in enumerate(decode(coded, layer)):
                out_ref[slot, :, 128 * c : 128 * c + 128] = piece


def body(grads, owned, left_stat, right_stat):
    shards, groups = lax.axis_size("shard"), lax.axis_size("dp")
    group = lax.axis_index("dp")
    blocks, strip, width = grads.shape[1:]
    core, chip, chips = group % 2, group // 2, groups // 2
    mine = lax.dynamic_index_in_dim(owned, group, 0, keepdims=False)
    square = jax.ShapeDtypeStruct((width, width), f32)
    halves = jax.ShapeDtypeStruct((width, width), bf16)
    wire = jax.ShapeDtypeStruct((shards * ROWS, 128), jnp.int16)
    grouped = grads[0].reshape(groups, shards, strip, width)
    swap = [(d, d ^ 1) for d in range(groups)]
    chunk = 8
    steps = shards // chunk
    half_wire = jax.ShapeDtypeStruct((shards * ROWS // 2, 128), jnp.int16)
    half_block = pl.BlockSpec((chunk * ROWS, 128), lambda i, *_: (i, 0))

    def cut(ahead, source):
        index = 2 * ((chip + ahead) % chips)
        return [lax.dynamic_index_in_dim(source, index + k, 0, keepdims=False) for k in (core, 1 - core)]

    def partner(array):
        return lax.ppermute(array, "dp", swap)

    def along(ahead, array):
        return lax.ppermute(array, "dp", [(d, (d + 2 * ahead) % groups) for d in range(groups)])

    def pair_sum(half, own, other, *parts):
        first = half * steps // 2
        strips_block = pl.BlockSpec((chunk, strip, width), lambda i: (i + first, 0, 0))
        return pl.pallas_call(
            pair_kernel,
            grid=(steps // 2,),
            in_specs=[strips_block] * 2 + [half_block] * len(parts),
            out_specs=half_block,
            out_shape=half_wire,
            compiler_params=params(),
            name=f"pair_{half}_{len(parts)}",
        )(own, other, *parts)

    held, far = lax.optimization_barrier((grouped, cut(2, grouped)))
    ahead, behind, mine_ = [cut(k, held) for k in (1, -1, 0)]
    for pair in (far, ahead, behind, mine_):
        pair[1] = partner(pair[1])
    left_relay = along(1, pair_sum(0, *far))
    right_relay = along(-1, pair_sum(1, *far))
    left_direct, right_direct = pair_sum(1, *ahead), pair_sum(0, *behind)
    ahead, behind, _, _ = lax.optimization_barrier((ahead, behind, left_direct, right_direct))
    left_direct, right_direct = along(1, left_direct), along(-1, right_direct)
    left_summed = along(1, pair_sum(0, *ahead, left_relay))
    right_summed = along(-1, pair_sum(1, *behind, right_relay))
    strips_block = pl.BlockSpec((chunk, strip, width), lambda i, *_: (i, 0, 0))
    lower = pl.BlockSpec((chunk * ROWS, 128), lambda i, *_: (jnp.minimum(i, steps // 2 - 1), 0))
    upper = pl.BlockSpec((chunk * ROWS, 128), lambda i, *_: (jnp.maximum(i - steps // 2, 0), 0))
    strips = pl.pallas_call(
        sum_kernel,
        grid_spec=pltpu.PrefetchScalarGridSpec(
            num_scalar_prefetch=1,
            grid=(steps,),
            in_specs=[strips_block, strips_block, lower, lower, upper, upper],
            out_specs=pl.BlockSpec((shards * ROWS, 128), lambda i, *_: (0, 0)),
            scratch_shapes=[
                pltpu.SMEM((shards,), jnp.int32),
                pltpu.VMEM((shards, ROWS, 128), jnp.int32),
                pltpu.VMEM((8, 128), f32),
            ],
        ),
        out_shape=wire,
        compiler_params=params(),
        name="sum_strips",
    )(mine, *mine_, left_summed, right_direct, left_direct, right_summed)
    strips = lax.all_to_all(strips, "shard", split_axis=0, concat_axis=0, tiled=True)
    high, low, left_fresh, left_root, sums = pl.pallas_call(
        left_kernel,
        in_specs=[VMEM, VMEM],
        out_specs=[VMEM] * 5,
        out_shape=[halves, halves, square, square, jax.ShapeDtypeStruct((16, 128), f32)],
        scratch_shapes=[pltpu.VMEM((width, width), f32)],
        compiler_params=params(),
        name="left",
    )(strips, left_stat[0, 0])
    pairs = [
        (((d + s) % groups) * shards + s, d * shards + s) for d in range(groups) for s in range(shards)
    ]
    total = lax.ppermute(sums[:8], ("dp", "shard"), pairs)
    right_fresh, right_root = pl.pallas_call(
        right_kernel,
        in_specs=[VMEM] * 3,
        out_specs=[VMEM] * 2,
        out_shape=[square, square],
        compiler_params=params(),
        cost_estimate=pl.CostEstimate(flops=10 * 2 * width**3, bytes_accessed=5 << 20, transcendentals=0),
        name="right",
    )(high, low, right_stat[0, 0])
    pieces = pl.pallas_call(
        shape_kernel,
        in_specs=[VMEM] * 6,
        out_specs=VMEM,
        out_shape=wire,
        scratch_shapes=[pltpu.VMEM((width, width), f32)],
        compiler_params=params(),
        name="shape",
    )(high, low, left_root, right_root, sums, total)
    pieces = lax.all_to_all(pieces, "shard", split_axis=0, concat_axis=0, tiled=True)
    update = pl.pallas_call(
        lambda *refs: update_kernel(groups, blocks * width * width, *refs),
        in_specs=[SMEM, VMEM],
        out_specs=VMEM,
        out_shape=jax.ShapeDtypeStruct((shards, strip, width), f32),
        compiler_params=params(),
        name="update",
    )(mine, pieces)
    return update, left_fresh[None, None], right_fresh[None, None]


def solution(mesh):
    return jax.shard_map(
        body,
        mesh=mesh,
        in_specs=(
            P("dp", None, "shard", None),
            P(),
            P("dp", "shard", None, None),
            P("dp", "shard", None, None),
        ),
        out_specs=(
            P("dp", "shard", None),
            P("dp", "shard", None, None),
            P("dp", "shard", None, None),
        ),
        check_vma=False,
    )
```

```python
import jax
import jax.numpy as jnp
from jax import lax
from jax.experimental import pallas as pl
from jax.experimental.pallas import tpu as pltpu
from jax.sharding import PartitionSpec as P

ROWS = 72
QUAD = 272
LIMIT = 32700.0
STEPS = 128.0
K = 1.25**6
EPS = 1e-06
f32, bf16 = jnp.float32, jnp.bfloat16
VMEM = pl.BlockSpec(memory_space=pltpu.VMEM)
SMEM = pl.BlockSpec(memory_space=pltpu.SMEM)
ANY = pl.BlockSpec(memory_space=pl.ANY)


def params(mebibytes):
    return pltpu.CompilerParams(vmem_limit_bytes=mebibytes << 20)


def upper_rows():
    return lax.broadcasted_iota(jnp.int32, (8, 128), 0) < 4


def encode_parts(strip):
    columns = [strip[:, c : c + 128] for c in range(0, strip.shape[1], 128)]
    top = jnp.abs(columns[0])
    for column in columns[1:]:
        top = jnp.maximum(top, jnp.abs(column))
    top = jnp.maximum(top[:8], top[8:])
    top = jnp.maximum(jnp.maximum(top, pltpu.roll(top, 4, 0)), 1e-30)
    code = jnp.ceil(jnp.log2(top) * STEPS)
    gain = jnp.exp2(code * (-1.0 / STEPS)) * LIMIT
    gain = jnp.concatenate([gain, gain], axis=0)
    return [jnp.round(column * gain) for column in columns], code


def encode(strip, number=None):
    coded, code = encode_parts(strip)
    tail = code if number is None else jnp.where(upper_rows(), code, number)
    return jnp.concatenate(coded + [tail], axis=0).astype(jnp.int32)


def encode_four(strips):
    coded, codes = zip(*[encode_parts(strip) for strip in strips])
    tails = [jnp.where(upper_rows(), codes[i], codes[i + 1]) for i in (0, 2)]
    return jnp.concatenate([c for part in coded for c in part] + tails, axis=0).astype(jnp.int32).astype(jnp.int16)


def decode_four(ref, quad):
    coded = ref[QUAD * quad : QUAD * (quad + 1), :].astype(jnp.int32).astype(f32)
    out = []
    for i in range(4):
        tail = coded[256 + 8 * (i // 2) : 264 + 8 * (i // 2)]
        gain = decode_gain(tail if i % 2 == 0 else pltpu.roll(tail, 4, 0))
        out.append([coded[r : r + 16] * gain for r in range(64 * i, 64 * i + 64, 16)])
    return out


def decode_gain(tail):
    code = jnp.where(upper_rows(), tail, pltpu.roll(tail, 4, 0))
    gain = jnp.exp2(code * (1.0 / STEPS)) * (1.0 / LIMIT)
    return jnp.concatenate([gain, gain], axis=0)


def decode(coded, factor=None):
    gain = decode_gain(coded[64:])
    if factor is not None:
        gain = gain * factor
    return [coded[r : r + 16] * gain for r in range(0, 64, 16)]


def load(ref, pair):
    both = ref[2 * ROWS * pair : 2 * ROWS * (pair + 1), :].astype(jnp.int32).astype(f32)
    return both[:ROWS], both[ROWS:]


def store(ref, pair, first, second):
    both = jnp.concatenate([first, second], axis=0)
    ref[2 * ROWS * pair : 2 * ROWS * (pair + 1), :] = both.astype(jnp.int16)


def encode_number(number):
    power = jnp.ceil(jnp.log2(jnp.maximum(number, 1e-30))) + 1.0
    digits = number * jnp.exp2(-power) * 16384.0
    high = jnp.floor(digits)
    low = jnp.floor((digits - high) * 16384.0)
    row = lax.broadcasted_iota(jnp.int32, number.shape, 0)
    return jnp.where(row == 4, power, jnp.where(row == 5, high, low))


def decode_number(tail):
    power, high, low = tail[4:5], tail[5:6], tail[6:7]
    return (high + low * (1.0 / 16384.0)) * (1.0 / 16384.0) * jnp.exp2(power)


def split(matrix):
    high = matrix.astype(bf16)
    return high, (matrix - high.astype(f32)).astype(bf16)


def dot3(left, right, dims=((1,), (0,))):
    dims = (dims, ((), ()))
    lh, ll = left
    rh, rl = right
    out = lax.dot_general(lh, rl, dims, preferred_element_type=f32)
    out += lax.dot_general(ll, rh, dims, preferred_element_type=f32)
    return out + lax.dot_general(lh, rh, dims, preferred_element_type=f32)


def eye_like(matrix):
    row = lax.broadcasted_iota(jnp.int32, matrix.shape, 0)
    column = lax.broadcasted_iota(jnp.int32, matrix.shape, 1)
    return row == column


def inverse_root(stat):
    diagonal = eye_like(stat)
    shifted = stat + jnp.where(diagonal, EPS, 0.0)
    norm = jnp.sqrt(jnp.sum(shifted * shifted, keepdims=True))
    u = shifted * (0.2 / norm)
    us = split(u)
    u2 = dot3(us, us)
    u2s = split(u2)
    rest = jnp.dot(u2s[0], (K * u2 - 5.0 * K * u).astype(bf16), preferred_element_type=f32)
    inner = 10.0 * K * (u2 - u) + rest
    outer = jnp.where(diagonal, 1.5625, 0.0) - (1.5625 + K) * u + 5.0 * K * u2
    root = outer + dot3(u2s, split(inner))
    return root * lax.rsqrt(jnp.sqrt(norm))


def invert(order_ref, slot_ref):
    def step(j, _):
        slot_ref[order_ref[j]] = j
        return 0

    lax.fori_loop(0, order_ref.shape[0], step, 0)


def cut_kernel(aheads, source_ref, *refs):
    group, (*outs, done) = lax.axis_index("dp"), refs
    chips = source_ref.shape[0] // 2
    copies = []
    for n, ahead in enumerate(aheads):
        base = 2 * ((group // 2 + ahead) % chips)
        for k, core in enumerate((group % 2, 1 - group % 2)):
            copies.append(pltpu.make_async_copy(source_ref.at[base + core], outs[2 * n + k], done.at[2 * n + k]))
    for copy in copies:
        copy.start()
    for copy in copies:
        copy.wait()


def pair_kernel(first, own_ref, other_ref, *refs):
    for q in range(refs[-1].shape[0] // QUAD):
        blocks = range(first + 4 * q, first + 4 * q + 4)
        strips = [own_ref[b].astype(f32) + other_ref[b].astype(f32) for b in blocks]
        if len(refs) > 1:
            parts = decode_four(refs[0], q)
            strips = [strip + jnp.concatenate(part, axis=1) for strip, part in zip(strips, parts)]
        refs[-1][QUAD * q : QUAD * (q + 1), :] = encode_four(strips)


def sum_kernel(order_ref, own_ref, other_ref, *refs):
    part_refs, (out_ref, square_ref, slot_ref, coded_ref) = refs[:4], refs[4:]
    invert(order_ref, slot_ref)
    total = jnp.zeros((8, 128), f32)
    quads = own_ref.shape[0] // 4
    for q in range(quads):
        lower = q < quads // 2
        parts = [decode_four(ref, q % (quads // 2)) for ref in (part_refs[:2] if lower else part_refs[2:])]
        for i in range(4):
            b = 4 * q + i
            strip = own_ref[b].astype(f32) + other_ref[b].astype(f32)
            first, second = [part[i] for part in parts]
            columns = [strip[:, 128 * c : 128 * c + 128] + (first[c] + second[c]) for c in range(4)]
            for column in columns:
                square = column * column
                total += square[:8] + square[8:]
            coded_ref[slot_ref[b]] = encode(jnp.concatenate(columns, axis=1))
    square_ref[...] = jnp.broadcast_to(jnp.sum(total, keepdims=True), total.shape)
    for p in range(coded_ref.shape[0] // 2):
        store(out_ref, p, coded_ref[2 * p], coded_ref[2 * p + 1])


def owner_kernel(coded_ref, left_in, right_in, total_ref, left_out, right_out, out_ref, *scratch):
    grad_ref, left_ref, right_ref, done = scratch
    order = grad_ref.shape[0]
    reads = [pltpu.make_async_copy(a, b, done.at[i]) for i, (a, b) in enumerate([(left_in, left_ref), (right_in, right_ref)])]
    for copy in reads:
        copy.start()
    square = jnp.zeros((16, 128), f32)
    for p in range(order // 32):
        for i, coded in enumerate(load(coded_ref, p)):
            row = 16 * (2 * p + i)
            for c, piece in enumerate(decode(coded)):
                square += piece * piece
                grad_ref[row : row + 16, 128 * c : 128 * c + 128] = piece
    grad = split(grad_ref[...])
    for copy in reads:
        copy.wait()
    left_ref[...] = 0.95 * left_ref[...] + dot3(grad, grad, ((1,), (1,))) * (1.0 / order)
    right_ref[...] = 0.95 * right_ref[...] + dot3(grad, grad, ((0,), (0,))) * (1.0 / order)
    writes = [pltpu.make_async_copy(a, b, done.at[i]) for i, (a, b) in enumerate([(left_ref, left_out), (right_ref, right_out)])]
    for copy in writes:
        copy.start()
    half = dot3(split(inverse_root(left_ref[...])), grad)
    shaped = dot3(split(half), split(inverse_root(right_ref[...])))
    cells = 1.0 / (order * order)
    mean = jnp.sum(shaped * shaped, keepdims=True) * cells
    graft = jnp.sqrt(jnp.sum(square, keepdims=True) * cells + EPS) / jnp.sqrt(mean + EPS)
    grad_ref[...] = shaped * graft
    number = encode_number(total_ref[...])
    for p in range(order // 32):
        rows = 32 * p
        store(
            out_ref,
            p,
            encode(grad_ref[rows : rows + 16, :], number),
            encode(grad_ref[rows + 16 : rows + 32, :], number),
        )
    for copy in writes:
        copy.wait()


def update_kernel(cells, order_ref, coded_ref, out_ref, wide_ref, done):
    total = jnp.zeros((1, 128), f32)
    for p in range(wide_ref.shape[0] // 2):
        base = 2 * ROWS * p
        first = coded_ref[base + 64 : base + 80, :].astype(jnp.int32).astype(f32)[:8]
        second = coded_ref[base + 128 : base + 144, :].astype(jnp.int32).astype(f32)[8:]
        total += decode_number(first) + decode_number(second)
    layer = 1.0 / jnp.sqrt(total * (1.0 / cells) + EPS)
    copies = []
    for p in range(wide_ref.shape[0] // 2):
        for i, coded in enumerate(load(coded_ref, p)):
            j = 2 * p + i
            for c, piece in enumerate(decode(coded, layer)):
                wide_ref[j, :, 128 * c : 128 * c + 128] = piece
            copies.append(pltpu.make_async_copy(wide_ref.at[j], out_ref.at[order_ref[j]], done.at[j]))
            copies[-1].start()
    for copy in copies:
        copy.wait()


def body(grads, owned, left_stat, right_stat):
    shards, groups = lax.axis_size("shard"), lax.axis_size("dp")
    group = lax.axis_index("dp")
    blocks, strip, width = grads.shape[1:]
    core, chip, chips = group % 2, group // 2, groups // 2
    mine = lax.dynamic_index_in_dim(owned, group, 0, keepdims=False)
    square = jax.ShapeDtypeStruct((width, width), f32)
    halves = jax.ShapeDtypeStruct((width, width), bf16)
    wire = jax.ShapeDtypeStruct((shards * ROWS, 128), jnp.int16)
    grouped = grads[0].reshape(groups, shards, strip, width)
    swap = [(d, d ^ 1) for d in range(groups)]
    half_wire = pltpu.VMEM((shards // 8 * QUAD, 128), jnp.int16)
    number = jax.ShapeDtypeStruct((8, 128), f32)

    def cut(source, *aheads):
        return pl.pallas_call(
            lambda *refs: cut_kernel([ahead % chips for ahead in aheads], *refs),
            in_specs=[pl.BlockSpec(memory_space=pltpu.HBM)],
            out_specs=[VMEM] * (2 * len(aheads)),
            out_shape=[pltpu.VMEM((shards, strip, width), bf16)] * (2 * len(aheads)),
            scratch_shapes=[pltpu.SemaphoreType.DMA((2 * len(aheads),))],
            compiler_params=params(4),
            name=f"cut_{len(aheads)}",
        )(source)

    def partner(array):
        return lax.ppermute(array, "dp", swap)

    def along(ahead, array):
        return lax.ppermute(array, "dp", [(d, (d + 2 * ahead) % groups) for d in range(groups)])

    def pair_sum(half, own, other, *parts):
        return pl.pallas_call(
            lambda *refs: pair_kernel(half * shards // 2, *refs),
            in_specs=[VMEM] * (2 + len(parts)),
            out_specs=VMEM,
            out_shape=half_wire,
            compiler_params=params(4),
            name=f"pair_{half}_{len(parts)}",
        )(own, other, *parts)

    held, far = lax.optimization_barrier((grouped, cut(grouped, 2)))
    far = far[0], partner(far[1])
    rest = cut(held, 1, -1, 0)
    others = [partner(rest[2 * n + 1]) for n in range(3)]
    left_relay, right_relay = pair_sum(0, *far), pair_sum(1, *far)
    owns, left_relay, right_relay = lax.optimization_barrier((rest[::2], left_relay, right_relay))
    ahead, behind, here = zip(owns, others)
    left_relay, right_relay = along(1, left_relay), along(-1, right_relay)
    left_direct, right_direct = pair_sum(1, *ahead), pair_sum(0, *behind)
    ahead, behind, _, _ = lax.optimization_barrier((ahead, behind, left_direct, right_direct))
    left_direct, right_direct = along(1, left_direct), along(-1, right_direct)
    left_summed = along(1, pair_sum(0, *ahead, left_relay))
    right_summed = along(-1, pair_sum(1, *behind, right_relay))
    strips, total = pl.pallas_call(
        sum_kernel,
        in_specs=[SMEM] + [VMEM] * 6,
        out_specs=[VMEM] * 2,
        scratch_shapes=[pltpu.SMEM((shards,), jnp.int32), pltpu.VMEM((shards, ROWS, 128), jnp.int32)],
        out_shape=[wire, number],
        compiler_params=params(8),
        name="sum_strips",
    )(mine, *here, left_summed, right_direct, left_direct, right_summed)
    strips = lax.all_to_all(strips, "shard", split_axis=0, concat_axis=0, tiled=True)
    for bit in (1, 2, 4):
        total += lax.ppermute(total, "dp", [(d, d ^ bit) for d in range(groups)])
    left_fresh, right_fresh, pieces = pl.pallas_call(
        owner_kernel,
        in_specs=[VMEM, ANY, ANY, VMEM],
        out_specs=[ANY, ANY, VMEM],
        out_shape=[square, square, wire],
        scratch_shapes=[pltpu.VMEM((width, width), f32)] * 3 + [pltpu.SemaphoreType.DMA((2,))],
        compiler_params=params(24),
        name="owner",
    )(strips, left_stat[0, 0], right_stat[0, 0], total)
    pieces = lax.all_to_all(pieces, "shard", split_axis=0, concat_axis=0, tiled=True)
    update = pl.pallas_call(
        lambda *refs: update_kernel(blocks * width * width, *refs),
        in_specs=[SMEM, VMEM],
        out_specs=ANY,
        out_shape=jax.ShapeDtypeStruct((shards, strip, width), f32),
        scratch_shapes=[pltpu.VMEM((shards, strip, width), f32), pltpu.SemaphoreType.DMA((shards,))],
        compiler_params=params(8),
        name="update",
    )(mine, pieces)
    return update, left_fresh[None, None], right_fresh[None, None]


def solution(mesh):
    return jax.shard_map(
        body,
        mesh=mesh,
        in_specs=(
            P("dp", None, "shard", None),
            P(),
            P("dp", "shard", None, None),
            P("dp", "shard", None, None),
        ),
        out_specs=(
            P("dp", "shard", None),
            P("dp", "shard", None, None),
            P("dp", "shard", None, None),
        ),
        check_vma=False,
    )
```

```python
import jax
import jax.numpy as jnp
from jax import lax
from jax.experimental import pallas as pl
from jax.experimental.pallas import tpu as pltpu
from jax.sharding import PartitionSpec as P

ROWS = 72
QUAD = 272
LIMIT = 32700.0
STEPS = 128.0
K = 1.25**6
EPS = 1e-06
f32, bf16 = jnp.float32, jnp.bfloat16
VMEM = pl.BlockSpec(memory_space=pltpu.VMEM)
SMEM = pl.BlockSpec(memory_space=pltpu.SMEM)
ANY = pl.BlockSpec(memory_space=pl.ANY)


def params(mebibytes):
    return pltpu.CompilerParams(vmem_limit_bytes=mebibytes << 20)


def upper_rows():
    return lax.broadcasted_iota(jnp.int32, (8, 128), 0) < 4


def encode_parts(strip, factor=None):
    columns = [strip[:, c : c + 128] for c in range(0, strip.shape[1], 128)]
    top = jnp.abs(columns[0])
    for column in columns[1:]:
        top = jnp.maximum(top, jnp.abs(column))
    top = jnp.maximum(top[:8], top[8:])
    top = jnp.maximum(top, pltpu.roll(top, 4, 0))
    top = jnp.maximum(top if factor is None else top * factor, 1e-30)
    code = jnp.ceil(jnp.log2(top) * STEPS)
    gain = jnp.exp2(code * (-1.0 / STEPS)) * LIMIT
    gain = gain if factor is None else gain * factor
    gain = jnp.concatenate([gain, gain], axis=0)
    return [jnp.round(column * gain) for column in columns], code


def encode(strip, number=None, factor=None):
    coded, code = encode_parts(strip, factor)
    tail = code if number is None else jnp.where(upper_rows(), code, number)
    return jnp.concatenate(coded + [tail], axis=0).astype(jnp.int32)


def encode_four(strips):
    coded, codes = zip(*[encode_parts(strip) for strip in strips])
    tails = [jnp.where(upper_rows(), codes[i], codes[i + 1]) for i in (0, 2)]
    return jnp.concatenate([c for part in coded for c in part] + tails, axis=0).astype(jnp.int32).astype(jnp.int16)


def decode_four(ref, quad):
    coded = ref[QUAD * quad : QUAD * (quad + 1), :].astype(jnp.int32).astype(f32)
    out = []
    for i in range(4):
        tail = coded[256 + 8 * (i // 2) : 264 + 8 * (i // 2)]
        gain = decode_gain(tail if i % 2 == 0 else pltpu.roll(tail, 4, 0))
        out.append([coded[r : r + 16] * gain for r in range(64 * i, 64 * i + 64, 16)])
    return out


def decode_gain(tail):
    code = jnp.where(upper_rows(), tail, pltpu.roll(tail, 4, 0))
    gain = jnp.exp2(code * (1.0 / STEPS)) * (1.0 / LIMIT)
    return jnp.concatenate([gain, gain], axis=0)


def decode(coded, factor=None):
    gain = decode_gain(coded[64:])
    if factor is not None:
        gain = gain * factor
    return [coded[r : r + 16] * gain for r in range(0, 64, 16)]


def load(ref, pair):
    both = ref[2 * ROWS * pair : 2 * ROWS * (pair + 1), :].astype(jnp.int32).astype(f32)
    return both[:ROWS], both[ROWS:]


def store(ref, pair, first, second):
    both = jnp.concatenate([first, second], axis=0)
    ref[2 * ROWS * pair : 2 * ROWS * (pair + 1), :] = both.astype(jnp.int16)


def encode_number(number):
    power = jnp.ceil(jnp.log2(jnp.maximum(number, 1e-30))) + 1.0
    digits = number * jnp.exp2(-power) * 16384.0
    high = jnp.floor(digits)
    low = jnp.floor((digits - high) * 16384.0)
    row = lax.broadcasted_iota(jnp.int32, number.shape, 0)
    return jnp.where(row == 4, power, jnp.where(row == 5, high, low))


def decode_number(tail):
    power, high, low = tail[4:5], tail[5:6], tail[6:7]
    return (high + low * (1.0 / 16384.0)) * (1.0 / 16384.0) * jnp.exp2(power)


def split(matrix):
    high = matrix.astype(bf16)
    return high, (matrix - high.astype(f32)).astype(bf16)


def dot3(left, right, dims=((1,), (0,))):
    (lh, ll), (rh, rl) = left, right
    axis = 1 - dims[0][0]
    rows = lh.shape[axis]
    dims = (dims, ((), ()))
    both = lax.dot_general(jnp.concatenate([lh, ll], axis=axis), rh, dims, preferred_element_type=f32)
    return both[:rows] + (both[rows:] + lax.dot_general(lh, rl, dims, preferred_element_type=f32))


def symmetric(left, right, dims=((1,), (0,)), product=None):
    product = product or dot3
    (rows,), (columns,) = (1 - dims[0][0],), (1 - dims[1][0],)
    half = left[0].shape[rows] // 2

    def part(pair, axis, start):
        return [lax.slice_in_dim(m, start, start + half, axis=axis) for m in pair]

    top = product(part(left, rows, 0), right, dims)
    corner = product(part(left, rows, half), part(right, columns, half), dims)
    lower = jnp.concatenate([top[:, half:].T, corner], axis=1)
    return jnp.concatenate([top, lower], axis=0)


def dot1(left, right, dims):
    return lax.dot_general(left[0], right[0], (dims, ((), ())), preferred_element_type=f32)


def eye_like(matrix):
    row = lax.broadcasted_iota(jnp.int32, matrix.shape, 0)
    column = lax.broadcasted_iota(jnp.int32, matrix.shape, 1)
    return row == column


def inverse_root(stat):
    diagonal = eye_like(stat)
    shifted = stat + jnp.where(diagonal, EPS, 0.0)
    norm = jnp.sqrt(jnp.sum(shifted * shifted, keepdims=True))
    u = shifted * (0.2 / norm)
    us = split(u)
    u2 = symmetric(us, us)
    u2s = split(u2)
    rest = symmetric(u2s, [(K * u2 - 5.0 * K * u).astype(bf16)], product=dot1)
    inner = 10.0 * K * (u2 - u) + rest
    outer = jnp.where(diagonal, 1.5625, 0.0) - (1.5625 + K) * u + 5.0 * K * u2
    root = outer + symmetric(u2s, split(inner))
    return root * lax.rsqrt(jnp.sqrt(norm))


def cut_kernel(wanted, source_ref, *refs):
    group, (*outs, done) = lax.axis_index("dp"), refs
    chips = source_ref.shape[0] // 2
    copies = []
    for n, (ahead, other) in enumerate(wanted):
        index = 2 * ((group // 2 + ahead) % chips) + (group % 2 + other) % 2
        copies.append(pltpu.make_async_copy(source_ref.at[index], outs[n], done.at[n]))
    for copy in copies:
        copy.start()
    for copy in copies:
        copy.wait()


def pair_kernel(first, own_ref, other_ref, *refs):
    for q in range(refs[-1].shape[0] // QUAD):
        blocks = range(first + 4 * q, first + 4 * q + 4)
        strips = [own_ref[b].astype(f32) + other_ref[b].astype(f32) for b in blocks]
        if len(refs) > 1:
            parts = decode_four(refs[0], q)
            strips = [strip + jnp.concatenate(part, axis=1) for strip, part in zip(strips, parts)]
        refs[-1][QUAD * q : QUAD * (q + 1), :] = encode_four(strips)


def sum_kernel(owned_ref, own_ref, other_ref, *refs):
    part_refs, (out_ref, square_ref, order_ref, coded_ref, done) = refs[:4], refs[4:]
    fetch = pltpu.make_async_copy(owned_ref.at[lax.axis_index("dp")], order_ref, done)
    fetch.start()
    total = jnp.zeros((8, 128), f32)
    quads = own_ref.shape[0] // 4
    for q in range(quads):
        lower = q < quads // 2
        parts = [decode_four(ref, q % (quads // 2)) for ref in (part_refs[:2] if lower else part_refs[2:])]
        for i in range(4):
            b = 4 * q + i
            strip = own_ref[b].astype(f32) + other_ref[b].astype(f32)
            first, second = [part[i] for part in parts]
            columns = [strip[:, 128 * c : 128 * c + 128] + (first[c] + second[c]) for c in range(4)]
            for column in columns:
                square = column * column
                total += square[:8] + square[8:]
            coded_ref[b] = encode(jnp.concatenate(columns, axis=1))
    square_ref[...] = jnp.broadcast_to(jnp.sum(total, keepdims=True), total.shape)
    fetch.wait()
    for p in range(coded_ref.shape[0] // 2):
        store(out_ref, p, coded_ref[order_ref[2 * p]], coded_ref[order_ref[2 * p + 1]])


def owner_kernel(coded_ref, left_in, right_in, total_ref, left_out, right_out, out_ref, *scratch):
    grad_ref, left_ref, right_ref, done = scratch
    order = grad_ref.shape[0]
    reads = [pltpu.make_async_copy(a, b, done.at[i]) for i, (a, b) in enumerate([(left_in, left_ref), (right_in, right_ref)])]
    for copy in reads:
        copy.start()
    square = jnp.zeros((16, 128), f32)
    for p in range(order // 32):
        for i, coded in enumerate(load(coded_ref, p)):
            row = 16 * (2 * p + i)
            for c, piece in enumerate(decode(coded)):
                square += piece * piece
                grad_ref[row : row + 16, 128 * c : 128 * c + 128] = piece
    grad = split(grad_ref[...])
    for copy in reads:
        copy.wait()
    left_ref[...] = 0.95 * left_ref[...] + symmetric(grad, grad, ((1,), (1,))) * (1.0 / order)
    right_ref[...] = 0.95 * right_ref[...] + symmetric(grad, grad, ((0,), (0,))) * (1.0 / order)
    writes = [pltpu.make_async_copy(a, b, done.at[i]) for i, (a, b) in enumerate([(left_ref, left_out), (right_ref, right_out)])]
    for copy in writes:
        copy.start()
    half = dot3(split(inverse_root(left_ref[...])), grad)
    shaped = dot3(split(half), split(inverse_root(right_ref[...])))
    cells = 1.0 / (order * order)
    mean = jnp.sum(shaped * shaped, keepdims=True) * cells
    graft = jnp.sqrt(jnp.sum(square, keepdims=True) * cells + EPS) / jnp.sqrt(mean + EPS)
    grad_ref[...] = shaped
    number = encode_number(total_ref[...])
    for p in range(order // 32):
        rows = 32 * p
        store(
            out_ref,
            p,
            encode(grad_ref[rows : rows + 16, :], number, graft),
            encode(grad_ref[rows + 16 : rows + 32, :], number, graft),
        )
    for copy in writes:
        copy.wait()


def add_kernel(first_ref, second_ref, out_ref):
    out_ref[...] = first_ref[...] + second_ref[...]


def update_kernel(cells, owned_ref, coded_ref, out_ref, order_ref, wide_ref, done, fetched):
    fetch = pltpu.make_async_copy(owned_ref.at[lax.axis_index("dp")], order_ref, fetched)
    fetch.start()
    total = jnp.zeros((1, 128), f32)
    for p in range(wide_ref.shape[0] // 2):
        base = 2 * ROWS * p
        first = coded_ref[base + 64 : base + 80, :].astype(jnp.int32).astype(f32)[:8]
        second = coded_ref[base + 128 : base + 144, :].astype(jnp.int32).astype(f32)[8:]
        total += decode_number(first) + decode_number(second)
    layer = 1.0 / jnp.sqrt(total * (1.0 / cells) + EPS)
    fetch.wait()
    copies = []
    for p in range(wide_ref.shape[0] // 2):
        for i, coded in enumerate(load(coded_ref, p)):
            j = 2 * p + i
            for c, piece in enumerate(decode(coded, layer)):
                wide_ref[j, :, 128 * c : 128 * c + 128] = piece
            copies.append(pltpu.make_async_copy(wide_ref.at[j], out_ref.at[order_ref[j]], done.at[j]))
            copies[-1].start()
    for copy in copies:
        copy.wait()


def body(grads, owned, left_stat, right_stat):
    shards, groups = lax.axis_size("shard"), lax.axis_size("dp")
    blocks, strip, width = grads.shape[1:]
    chips = groups // 2
    square = jax.ShapeDtypeStruct((width, width), f32)
    wire = jax.ShapeDtypeStruct((shards * ROWS, 128), jnp.int16)
    grouped = grads[0].reshape(groups, shards, strip, width)
    swap = [(d, d ^ 1) for d in range(groups)]
    half_wire = pltpu.VMEM((shards // 8 * QUAD, 128), jnp.int16)
    number = jax.ShapeDtypeStruct((8, 128), f32)

    def cut(mebibytes, source, *wanted):
        return pl.pallas_call(
            lambda *refs: cut_kernel([(ahead % chips, other) for ahead, other in wanted], *refs),
            in_specs=[ANY],
            out_specs=[VMEM] * len(wanted),
            out_shape=[pltpu.VMEM((shards, strip, width), bf16)] * len(wanted),
            scratch_shapes=[pltpu.SemaphoreType.DMA((len(wanted),))],
            compiler_params=params(mebibytes),
            name=f"cut_{len(wanted)}",
        )(source)

    def partner(array):
        return lax.ppermute(array, "dp", swap)

    def along(ahead, array):
        return lax.ppermute(array, "dp", [(d, (d + 2 * ahead) % groups) for d in range(groups)])

    def pair_sum(half, own, other, *parts):
        return pl.pallas_call(
            lambda *refs: pair_kernel(half * shards // 2, *refs),
            in_specs=[VMEM] * (2 + len(parts)),
            out_specs=VMEM,
            out_shape=half_wire,
            compiler_params=params(4),
            name=f"pair_{half}_{len(parts)}",
        )(own, other, *parts)

    held, far = lax.optimization_barrier((grouped, cut(60, grouped, (2, 1))))
    far = partner(*far)
    own, *rest = cut(57, held, (2, 0), (1, 1), (-1, 1), (0, 1), (1, 0), (-1, 0), (0, 0))
    others = [partner(array) for array in rest[:3]]
    left_relay, right_relay = pair_sum(0, own, far), pair_sum(1, own, far)
    owns, left_relay, right_relay = lax.optimization_barrier((rest[3:], left_relay, right_relay))
    ahead, behind, here = zip(owns, others)
    left_relay, right_relay = along(1, left_relay), along(-1, right_relay)
    left_direct, right_direct = pair_sum(1, *ahead), pair_sum(0, *behind)
    ahead, behind, _, _ = lax.optimization_barrier((ahead, behind, left_direct, right_direct))
    left_direct, right_direct = along(1, left_direct), along(-1, right_direct)
    left_summed = along(1, pair_sum(0, *ahead, left_relay))
    right_summed = along(-1, pair_sum(1, *behind, right_relay))
    strips, total = pl.pallas_call(
        sum_kernel,
        in_specs=[ANY] + [VMEM] * 6,
        out_specs=[VMEM] * 2,
        scratch_shapes=[
            pltpu.SMEM((shards,), jnp.int32),
            pltpu.VMEM((shards, ROWS, 128), jnp.int32),
            pltpu.SemaphoreType.DMA,
        ],
        out_shape=[pltpu.VMEM(wire.shape, wire.dtype), number],
        compiler_params=params(8),
        name="sum_strips",
    )(owned, *here, left_summed, right_direct, left_direct, right_summed)
    strips = lax.all_to_all(strips, "shard", split_axis=0, concat_axis=0, tiled=True)
    for bit in (1, 2, 4):
        other = lax.ppermute(total, "dp", [(d, d ^ bit) for d in range(groups)])
        total = pl.pallas_call(
            add_kernel,
            in_specs=[VMEM] * 2,
            out_specs=VMEM,
            out_shape=number,
            compiler_params=params(1),
            name=f"add_{bit}",
        )(total, other)
    left_fresh, right_fresh, pieces = pl.pallas_call(
        owner_kernel,
        in_specs=[VMEM, ANY, ANY, VMEM],
        out_specs=[ANY, ANY, VMEM],
        out_shape=[square, square, wire],
        scratch_shapes=[pltpu.VMEM((width, width), f32)] * 3 + [pltpu.SemaphoreType.DMA((2,))],
        compiler_params=params(24),
        name="owner",
    )(strips, left_stat[0, 0], right_stat[0, 0], total)
    pieces = lax.all_to_all(pieces, "shard", split_axis=0, concat_axis=0, tiled=True)
    update = pl.pallas_call(
        lambda *refs: update_kernel(blocks * width * width, *refs),
        in_specs=[ANY, VMEM],
        out_specs=ANY,
        out_shape=jax.ShapeDtypeStruct((shards, strip, width), f32),
        scratch_shapes=[
            pltpu.SMEM((shards,), jnp.int32),
            pltpu.VMEM((shards, strip, width), f32),
            pltpu.SemaphoreType.DMA((shards,)),
            pltpu.SemaphoreType.DMA,
        ],
        compiler_params=params(8),
        name="update",
    )(owned, pieces)
    return update, left_fresh[None, None], right_fresh[None, None]


def solution(mesh):
    return jax.shard_map(
        body,
        mesh=mesh,
        in_specs=(
            P("dp", None, "shard", None),
            P(),
            P("dp", "shard", None, None),
            P("dp", "shard", None, None),
        ),
        out_specs=(
            P("dp", "shard", None),
            P("dp", "shard", None, None),
            P("dp", "shard", None, None),
        ),
        check_vma=False,
    )
```

```python
import jax
import jax.numpy as jnp
from jax import lax
from jax.experimental import pallas as pl
from jax.experimental.pallas import tpu as pltpu
from jax.sharding import PartitionSpec as P

ROWS = 72
QUAD = 272
LIMIT = 32700.0
STEPS = 128.0
K = 1.25**6
EPS = 1e-06
f32, bf16 = jnp.float32, jnp.bfloat16
VMEM = pl.BlockSpec(memory_space=pltpu.VMEM)
SMEM = pl.BlockSpec(memory_space=pltpu.SMEM)
ANY = pl.BlockSpec(memory_space=pl.ANY)


def params(mebibytes):
    return pltpu.CompilerParams(vmem_limit_bytes=mebibytes << 20)


def upper_rows():
    return lax.broadcasted_iota(jnp.int32, (8, 128), 0) < 4


def encode_parts(strip, factor=None):
    columns = [strip[:, c : c + 128] for c in range(0, strip.shape[1], 128)]
    top = jnp.abs(columns[0])
    for column in columns[1:]:
        top = jnp.maximum(top, jnp.abs(column))
    top = jnp.maximum(top[:8], top[8:])
    top = jnp.maximum(top, pltpu.roll(top, 4, 0))
    top = jnp.maximum(top if factor is None else top * factor, 1e-30)
    code = jnp.ceil(jnp.log2(top) * STEPS)
    gain = jnp.exp2(code * (-1.0 / STEPS)) * LIMIT
    gain = gain if factor is None else gain * factor
    gain = jnp.concatenate([gain, gain], axis=0)
    return [jnp.round(column * gain) for column in columns], code


def encode(strip, number=None, factor=None):
    coded, code = encode_parts(strip, factor)
    tail = code if number is None else jnp.where(upper_rows(), code, number)
    return jnp.concatenate(coded + [tail], axis=0).astype(jnp.int32)


def encode_four(strips):
    coded, codes = zip(*[encode_parts(strip) for strip in strips])
    tails = [jnp.where(upper_rows(), codes[i], codes[i + 1]) for i in (0, 2)]
    return jnp.concatenate([c for part in coded for c in part] + tails, axis=0).astype(jnp.int32).astype(jnp.int16)


def decode_four(ref, quad):
    coded = ref[QUAD * quad : QUAD * (quad + 1), :].astype(jnp.int32).astype(f32)
    out = []
    for i in range(4):
        tail = coded[256 + 8 * (i // 2) : 264 + 8 * (i // 2)]
        gain = decode_gain(tail if i % 2 == 0 else pltpu.roll(tail, 4, 0))
        out.append([coded[r : r + 16] * gain for r in range(64 * i, 64 * i + 64, 16)])
    return out


def decode_gain(tail):
    code = jnp.where(upper_rows(), tail, pltpu.roll(tail, 4, 0))
    gain = jnp.exp2(code * (1.0 / STEPS)) * (1.0 / LIMIT)
    return jnp.concatenate([gain, gain], axis=0)


def decode(coded, factor=None):
    gain = decode_gain(coded[64:])
    if factor is not None:
        gain = gain * factor
    return [coded[r : r + 16] * gain for r in range(0, 64, 16)]


def load(ref, pair):
    both = ref[2 * ROWS * pair : 2 * ROWS * (pair + 1), :].astype(jnp.int32).astype(f32)
    return both[:ROWS], both[ROWS:]


def store(ref, pair, first, second):
    both = jnp.concatenate([first, second], axis=0)
    ref[2 * ROWS * pair : 2 * ROWS * (pair + 1), :] = both.astype(jnp.int16)


def encode_number(number):
    power = jnp.ceil(jnp.log2(jnp.maximum(number, 1e-30))) + 1.0
    digits = number * jnp.exp2(-power) * 16384.0
    high = jnp.floor(digits)
    low = jnp.floor((digits - high) * 16384.0)
    row = lax.broadcasted_iota(jnp.int32, number.shape, 0)
    return jnp.where(row == 4, power, jnp.where(row == 5, high, low))


def decode_number(tail):
    power, high, low = tail[4:5], tail[5:6], tail[6:7]
    return (high + low * (1.0 / 16384.0)) * (1.0 / 16384.0) * jnp.exp2(power)


def split(matrix):
    high = matrix.astype(bf16)
    return high, (matrix - high.astype(f32)).astype(bf16)


def dot3(left, right, dims=((1,), (0,))):
    (lh, ll), (rh, rl) = left, right
    axis = 1 - dims[0][0]
    rows = lh.shape[axis]
    dims = (dims, ((), ()))
    both = lax.dot_general(jnp.concatenate([lh, ll], axis=axis), rh, dims, preferred_element_type=f32)
    return both[:rows] + (both[rows:] + lax.dot_general(lh, rl, dims, preferred_element_type=f32))


def symmetric(left, right, dims=((1,), (0,)), product=None):
    product = product or dot3
    (rows,), (columns,) = (1 - dims[0][0],), (1 - dims[1][0],)
    half = left[0].shape[rows] // 2

    def part(pair, axis, start):
        return [lax.slice_in_dim(m, start, start + half, axis=axis) for m in pair]

    top = product(part(left, rows, 0), right, dims)
    corner = product(part(left, rows, half), part(right, columns, half), dims)
    lower = jnp.concatenate([top[:, half:].T, corner], axis=1)
    return jnp.concatenate([top, lower], axis=0)


def dot1(left, right, dims):
    return lax.dot_general(left[0], right[0], (dims, ((), ())), preferred_element_type=f32)


def eye_like(matrix):
    row = lax.broadcasted_iota(jnp.int32, matrix.shape, 0)
    column = lax.broadcasted_iota(jnp.int32, matrix.shape, 1)
    return row == column


def inverse_root(stat):
    diagonal = eye_like(stat)
    shifted = stat + jnp.where(diagonal, EPS, 0.0)
    norm = jnp.sqrt(jnp.sum(shifted * shifted, keepdims=True))
    u = shifted * (0.2 / norm)
    us = split(u)
    u2 = symmetric(us, us)
    u2s = split(u2)
    rest = symmetric(u2s, [(K * u2 - 5.0 * K * u).astype(bf16)], product=dot1)
    inner = 10.0 * K * (u2 - u) + rest
    outer = jnp.where(diagonal, 1.5625, 0.0) - (1.5625 + K) * u + 5.0 * K * u2
    root = outer + symmetric(u2s, split(inner))
    return root * lax.rsqrt(jnp.sqrt(norm))


def cut_kernel(wanted, source_ref, *refs):
    group, (*outs, done) = lax.axis_index("dp"), refs
    chips = source_ref.shape[0] // 2
    copies = []
    for n, (ahead, other) in enumerate(wanted):
        index = 2 * ((group // 2 + ahead) % chips) + (group % 2 + other) % 2
        copies.append(pltpu.make_async_copy(source_ref.at[index], outs[n], done.at[n]))
    for copy in copies:
        copy.start()
    for copy in copies:
        copy.wait()


def pair_kernel(first, own_ref, other_ref, *refs):
    for q in range(refs[-1].shape[0] // QUAD):
        blocks = range(first + 4 * q, first + 4 * q + 4)
        strips = [own_ref[b].astype(f32) + other_ref[b].astype(f32) for b in blocks]
        if len(refs) > 1:
            parts = decode_four(refs[0], q)
            strips = [strip + jnp.concatenate(part, axis=1) for strip, part in zip(strips, parts)]
        refs[-1][QUAD * q : QUAD * (q + 1), :] = encode_four(strips)


def sum_kernel(owned_ref, own_ref, other_ref, *refs):
    part_refs, (out_ref, square_ref, order_ref, coded_ref, packed_ref, done, sent) = refs[:4], refs[4:]
    fetch = pltpu.make_async_copy(owned_ref.at[lax.axis_index("dp")], order_ref, done)
    fetch.start()
    total = jnp.zeros((8, 128), f32)
    quads = own_ref.shape[0] // 4
    for q in range(quads):
        lower = q < quads // 2
        parts = [decode_four(ref, q % (quads // 2)) for ref in (part_refs[:2] if lower else part_refs[2:])]
        for i in range(4):
            b = 4 * q + i
            strip = own_ref[b].astype(f32) + other_ref[b].astype(f32)
            first, second = [part[i] for part in parts]
            columns = [strip[:, 128 * c : 128 * c + 128] + (first[c] + second[c]) for c in range(4)]
            for column in columns:
                square = column * column
                total += square[:8] + square[8:]
            coded_ref[b] = encode(jnp.concatenate(columns, axis=1))
    square_ref[...] = jnp.broadcast_to(jnp.sum(total, keepdims=True), total.shape)
    fetch.wait()
    copies = []
    for p in range(coded_ref.shape[0] // 2):
        store(packed_ref, p, coded_ref[order_ref[2 * p]], coded_ref[order_ref[2 * p + 1]])
        if p % 4 == 3:
            rows = pl.ds(2 * ROWS * (p - 3), 8 * ROWS)
            copies.append(pltpu.make_async_copy(packed_ref.at[rows], out_ref.at[rows], sent.at[p // 4]))
            copies[-1].start()
    for copy in copies:
        copy.wait()


def owner_kernel(coded_ref, left_in, right_in, total_ref, left_out, right_out, out_ref, *scratch):
    grad_ref, left_ref, right_ref, done = scratch
    order = grad_ref.shape[0]
    reads = [pltpu.make_async_copy(a, b, done.at[i]) for i, (a, b) in enumerate([(left_in, left_ref), (right_in, right_ref)])]
    for copy in reads:
        copy.start()
    square = jnp.zeros((16, 128), f32)
    for p in range(order // 32):
        for i, coded in enumerate(load(coded_ref, p)):
            row = 16 * (2 * p + i)
            for c, piece in enumerate(decode(coded)):
                square += piece * piece
                grad_ref[row : row + 16, 128 * c : 128 * c + 128] = piece
    grad = split(grad_ref[...])
    for copy in reads:
        copy.wait()
    left_ref[...] = 0.95 * left_ref[...] + symmetric(grad, grad, ((1,), (1,))) * (1.0 / order)
    right_ref[...] = 0.95 * right_ref[...] + symmetric(grad, grad, ((0,), (0,))) * (1.0 / order)
    writes = [pltpu.make_async_copy(a, b, done.at[i]) for i, (a, b) in enumerate([(left_ref, left_out), (right_ref, right_out)])]
    for copy in writes:
        copy.start()
    half = dot3(split(inverse_root(left_ref[...])), grad)
    shaped = dot3(split(half), split(inverse_root(right_ref[...])))
    cells = 1.0 / (order * order)
    mean = jnp.sum(shaped * shaped, keepdims=True) * cells
    graft = jnp.sqrt(jnp.sum(square, keepdims=True) * cells + EPS) / jnp.sqrt(mean + EPS)
    grad_ref[...] = shaped
    number = encode_number(total_ref[...])
    for p in range(order // 32):
        rows = 32 * p
        store(
            out_ref,
            p,
            encode(grad_ref[rows : rows + 16, :], number, graft),
            encode(grad_ref[rows + 16 : rows + 32, :], number, graft),
        )
    for copy in writes:
        copy.wait()


def add_kernel(first_ref, second_ref, out_ref):
    out_ref[...] = first_ref[...] + second_ref[...]


def update_kernel(cells, owned_ref, coded_ref, out_ref, order_ref, wide_ref, done, fetched):
    fetch = pltpu.make_async_copy(owned_ref.at[lax.axis_index("dp")], order_ref, fetched)
    fetch.start()
    total = jnp.zeros((1, 128), f32)
    for p in range(wide_ref.shape[0] // 2):
        base = 2 * ROWS * p
        first = coded_ref[base + 64 : base + 80, :].astype(jnp.int32).astype(f32)[:8]
        second = coded_ref[base + 128 : base + 144, :].astype(jnp.int32).astype(f32)[8:]
        total += decode_number(first) + decode_number(second)
    layer = 1.0 / jnp.sqrt(total * (1.0 / cells) + EPS)
    fetch.wait()
    copies = []
    for p in range(wide_ref.shape[0] // 2):
        for i, coded in enumerate(load(coded_ref, p)):
            j = 2 * p + i
            for c, piece in enumerate(decode(coded, layer)):
                wide_ref[j, :, 128 * c : 128 * c + 128] = piece
            copies.append(pltpu.make_async_copy(wide_ref.at[j], out_ref.at[order_ref[j]], done.at[j]))
            copies[-1].start()
    for copy in copies:
        copy.wait()


def body(grads, owned, left_stat, right_stat):
    shards, groups = lax.axis_size("shard"), lax.axis_size("dp")
    blocks, strip, width = grads.shape[1:]
    chips = groups // 2
    square = jax.ShapeDtypeStruct((width, width), f32)
    wire = jax.ShapeDtypeStruct((shards * ROWS, 128), jnp.int16)
    grouped = grads[0].reshape(groups, shards, strip, width)
    swap = [(d, d ^ 1) for d in range(groups)]
    half_wire = pltpu.VMEM((shards // 8 * QUAD, 128), jnp.int16)
    number = jax.ShapeDtypeStruct((8, 128), f32)

    def cut(mebibytes, source, *wanted):
        return pl.pallas_call(
            lambda *refs: cut_kernel([(ahead % chips, other) for ahead, other in wanted], *refs),
            in_specs=[ANY],
            out_specs=[VMEM] * len(wanted),
            out_shape=[pltpu.VMEM((shards, strip, width), bf16)] * len(wanted),
            scratch_shapes=[pltpu.SemaphoreType.DMA((len(wanted),))],
            compiler_params=params(mebibytes),
            name=f"cut_{len(wanted)}",
        )(source)

    def partner(array):
        return lax.ppermute(array, "dp", swap)

    def along(ahead, array):
        return lax.ppermute(array, "dp", [(d, (d + 2 * ahead) % groups) for d in range(groups)])

    def pair_sum(half, own, other, *parts):
        return pl.pallas_call(
            lambda *refs: pair_kernel(half * shards // 2, *refs),
            in_specs=[VMEM] * (2 + len(parts)),
            out_specs=VMEM,
            out_shape=half_wire,
            compiler_params=params(4),
            name=f"pair_{half}_{len(parts)}",
        )(own, other, *parts)

    held, far = lax.optimization_barrier((grouped, cut(60, grouped, (2, 1))))
    far = partner(*far)
    own, *rest = cut(57, held, (2, 0), (1, 1), (-1, 1), (0, 1), (1, 0), (-1, 0), (0, 0))
    others = [partner(array) for array in rest[:3]]
    left_relay, right_relay = pair_sum(0, own, far), pair_sum(1, own, far)
    owns, left_relay, right_relay = lax.optimization_barrier((rest[3:], left_relay, right_relay))
    ahead, behind, here = zip(owns, others)
    left_relay, right_relay = along(1, left_relay), along(-1, right_relay)
    left_direct, right_direct = pair_sum(1, *ahead), pair_sum(0, *behind)
    left_direct = along(1, left_direct)
    left_summed, right_summed = pair_sum(0, *ahead, left_relay), pair_sum(1, *behind, right_relay)
    left_summed, right_summed, right_direct = lax.optimization_barrier((left_summed, right_summed, right_direct))
    left_summed, right_summed = along(1, left_summed), along(-1, right_summed)
    right_direct = along(-1, right_direct)
    strips, total = pl.pallas_call(
        sum_kernel,
        in_specs=[ANY] + [VMEM] * 6,
        out_specs=[ANY, VMEM],
        scratch_shapes=[
            pltpu.SMEM((shards,), jnp.int32),
            pltpu.VMEM((shards, ROWS, 128), jnp.int32),
            pltpu.VMEM(wire.shape, wire.dtype),
            pltpu.SemaphoreType.DMA,
            pltpu.SemaphoreType.DMA((shards // 8,)),
        ],
        out_shape=[wire, number],
        compiler_params=params(8),
        name="sum_strips",
    )(owned, *here, left_summed, right_direct, left_direct, right_summed)
    strips = lax.all_to_all(strips, "shard", split_axis=0, concat_axis=0, tiled=True)
    for bit in (1, 2, 4):
        other = lax.ppermute(total, "dp", [(d, d ^ bit) for d in range(groups)])
        total = pl.pallas_call(
            add_kernel,
            in_specs=[VMEM] * 2,
            out_specs=VMEM,
            out_shape=number,
            compiler_params=params(1),
            name=f"add_{bit}",
        )(total, other)
    left_fresh, right_fresh, pieces = pl.pallas_call(
        owner_kernel,
        in_specs=[VMEM, ANY, ANY, VMEM],
        out_specs=[ANY, ANY, VMEM],
        out_shape=[square, square, wire],
        scratch_shapes=[pltpu.VMEM((width, width), f32)] * 3 + [pltpu.SemaphoreType.DMA((2,))],
        compiler_params=params(24),
        name="owner",
    )(strips, left_stat[0, 0], right_stat[0, 0], total)
    pieces = lax.all_to_all(pieces, "shard", split_axis=0, concat_axis=0, tiled=True)
    update = pl.pallas_call(
        lambda *refs: update_kernel(blocks * width * width, *refs),
        in_specs=[ANY, VMEM],
        out_specs=ANY,
        out_shape=jax.ShapeDtypeStruct((shards, strip, width), f32),
        scratch_shapes=[
            pltpu.SMEM((shards,), jnp.int32),
            pltpu.VMEM((shards, strip, width), f32),
            pltpu.SemaphoreType.DMA((shards,)),
            pltpu.SemaphoreType.DMA,
        ],
        compiler_params=params(8),
        name="update",
    )(owned, pieces)
    return update, left_fresh[None, None], right_fresh[None, None]


def solution(mesh):
    return jax.shard_map(
        body,
        mesh=mesh,
        in_specs=(
            P("dp", None, "shard", None),
            P(),
            P("dp", "shard", None, None),
            P("dp", "shard", None, None),
        ),
        out_specs=(
            P("dp", "shard", None),
            P("dp", "shard", None, None),
            P("dp", "shard", None, None),
        ),
        check_vma=False,
    )
```

```python
import jax
import jax.numpy as jnp
from jax import lax
from jax.experimental import pallas as pl
from jax.experimental.pallas import tpu as pltpu
from jax.sharding import PartitionSpec as P

ROWS = 72
QUAD = 272
LIMIT = 32700.0
STEPS = 128.0
K = 1.25**6
EPS = 1e-06
f32, bf16 = jnp.float32, jnp.bfloat16
VMEM = pl.BlockSpec(memory_space=pltpu.VMEM)
SMEM = pl.BlockSpec(memory_space=pltpu.SMEM)
ANY = pl.BlockSpec(memory_space=pl.ANY)


def params(mebibytes):
    return pltpu.CompilerParams(vmem_limit_bytes=mebibytes << 20)


def upper_rows():
    return lax.broadcasted_iota(jnp.int32, (8, 128), 0) < 4


def encode_parts(strip, factor=None):
    columns = [strip[:, c : c + 128] for c in range(0, strip.shape[1], 128)]
    top = jnp.abs(columns[0])
    for column in columns[1:]:
        top = jnp.maximum(top, jnp.abs(column))
    top = jnp.maximum(top[:8], top[8:])
    top = jnp.maximum(top, pltpu.roll(top, 4, 0))
    top = jnp.maximum(top if factor is None else top * factor, 1e-30)
    code = jnp.ceil(jnp.log2(top) * STEPS)
    gain = jnp.exp2(code * (-1.0 / STEPS)) * LIMIT
    gain = gain if factor is None else gain * factor
    gain = jnp.concatenate([gain, gain], axis=0)
    return [jnp.round(column * gain) for column in columns], code


def encode(strip, number=None, factor=None):
    coded, code = encode_parts(strip, factor)
    tail = code if number is None else jnp.where(upper_rows(), code, number)
    return jnp.concatenate(coded + [tail], axis=0).astype(jnp.int32)


def encode_four(strips):
    coded, codes = zip(*[encode_parts(strip) for strip in strips])
    tails = [jnp.where(upper_rows(), codes[i], codes[i + 1]) for i in (0, 2)]
    return jnp.concatenate([c for part in coded for c in part] + tails, axis=0).astype(jnp.int32).astype(jnp.int16)


def decode_four(ref, quad):
    coded = ref[QUAD * quad : QUAD * (quad + 1), :].astype(jnp.int32).astype(f32)
    out = []
    for i in range(4):
        tail = coded[256 + 8 * (i // 2) : 264 + 8 * (i // 2)]
        gain = decode_gain(tail if i % 2 == 0 else pltpu.roll(tail, 4, 0))
        out.append([coded[r : r + 16] * gain for r in range(64 * i, 64 * i + 64, 16)])
    return out


def decode_gain(tail):
    code = jnp.where(upper_rows(), tail, pltpu.roll(tail, 4, 0))
    gain = jnp.exp2(code * (1.0 / STEPS)) * (1.0 / LIMIT)
    return jnp.concatenate([gain, gain], axis=0)


def decode(coded, factor=None):
    gain = decode_gain(coded[64:])
    if factor is not None:
        gain = gain * factor
    return [coded[r : r + 16] * gain for r in range(0, 64, 16)]


def load(ref, pair):
    both = ref[2 * ROWS * pair : 2 * ROWS * (pair + 1), :].astype(jnp.int32).astype(f32)
    return both[:ROWS], both[ROWS:]


def store(ref, pair, first, second):
    both = jnp.concatenate([first, second], axis=0)
    ref[2 * ROWS * pair : 2 * ROWS * (pair + 1), :] = both.astype(jnp.int16)


def encode_number(number):
    power = jnp.ceil(jnp.log2(jnp.maximum(number, 1e-30))) + 1.0
    digits = number * jnp.exp2(-power) * 16384.0
    high = jnp.floor(digits)
    low = jnp.floor((digits - high) * 16384.0)
    row = lax.broadcasted_iota(jnp.int32, number.shape, 0)
    return jnp.where(row == 4, power, jnp.where(row == 5, high, low))


def decode_number(tail):
    power, high, low = tail[4:5], tail[5:6], tail[6:7]
    return (high + low * (1.0 / 16384.0)) * (1.0 / 16384.0) * jnp.exp2(power)


def split(matrix):
    high = matrix.astype(bf16)
    return high, (matrix - high.astype(f32)).astype(bf16)


def dot3(left, right, dims=((1,), (0,))):
    (lh, ll), (rh, rl) = left, right
    axis = 1 - dims[0][0]
    rows = lh.shape[axis]
    dims = (dims, ((), ()))
    both = lax.dot_general(jnp.concatenate([lh, ll], axis=axis), rh, dims, preferred_element_type=f32)
    return both[:rows] + (both[rows:] + lax.dot_general(lh, rl, dims, preferred_element_type=f32))


def symmetric(left, right, dims=((1,), (0,)), product=None):
    product = product or dot3
    (rows,), (columns,) = (1 - dims[0][0],), (1 - dims[1][0],)
    half = left[0].shape[rows] // 2

    def part(pair, axis, start):
        return [lax.slice_in_dim(m, start, start + half, axis=axis) for m in pair]

    top = product(part(left, rows, 0), right, dims)
    corner = product(part(left, rows, half), part(right, columns, half), dims)
    lower = jnp.concatenate([top[:, half:].T, corner], axis=1)
    return jnp.concatenate([top, lower], axis=0)


def dot1(left, right, dims):
    return lax.dot_general(left[0], right[0], (dims, ((), ())), preferred_element_type=f32)


def eye_like(matrix):
    row = lax.broadcasted_iota(jnp.int32, matrix.shape, 0)
    column = lax.broadcasted_iota(jnp.int32, matrix.shape, 1)
    return row == column


def inverse_root(stat):
    diagonal = eye_like(stat)
    shifted = stat + jnp.where(diagonal, EPS, 0.0)
    norm = jnp.sqrt(jnp.sum(shifted * shifted, keepdims=True))
    u = shifted * (0.2 / norm)
    us = split(u)
    u2 = symmetric(us, us)
    u2s = split(u2)
    rest = symmetric(u2s, [(K * u2 - 5.0 * K * u).astype(bf16)], product=dot1)
    inner = 10.0 * K * (u2 - u) + rest
    outer = jnp.where(diagonal, 1.5625, 0.0) - (1.5625 + K) * u + 5.0 * K * u2
    root = outer + symmetric(u2s, split(inner))
    return root * lax.rsqrt(jnp.sqrt(norm))


def cut_kernel(wanted, source_ref, *refs):
    group, (*outs, done) = lax.axis_index("dp"), refs
    chips = source_ref.shape[0] // 2
    copies = []
    for n, (ahead, other) in enumerate(wanted):
        index = 2 * ((group // 2 + ahead) % chips) + (group % 2 + other) % 2
        copies.append(pltpu.make_async_copy(source_ref.at[index], outs[n], done.at[n]))
    for copy in copies:
        copy.start()
    for copy in copies:
        copy.wait()


def pair_kernel(first, own_ref, other_ref, *refs):
    for q in range(refs[-1].shape[0] // QUAD):
        blocks = range(first + 4 * q, first + 4 * q + 4)
        strips = [own_ref[b].astype(f32) + other_ref[b].astype(f32) for b in blocks]
        if len(refs) > 1:
            parts = decode_four(refs[0], q)
            strips = [strip + jnp.concatenate(part, axis=1) for strip, part in zip(strips, parts)]
        refs[-1][QUAD * q : QUAD * (q + 1), :] = encode_four(strips)


def sum_kernel(owned_ref, own_ref, other_ref, *refs):
    part_refs, (out_ref, square_ref, order_ref, coded_ref, packed_ref, done, sent) = refs[:4], refs[4:]
    fetch = pltpu.make_async_copy(owned_ref.at[lax.axis_index("dp")], order_ref, done)
    fetch.start()
    total = jnp.zeros((8, 128), f32)
    quads = own_ref.shape[0] // 4
    for q in range(quads):
        lower = q < quads // 2
        parts = [decode_four(ref, q % (quads // 2)) for ref in (part_refs[:2] if lower else part_refs[2:])]
        for i in range(4):
            b = 4 * q + i
            strip = own_ref[b].astype(f32) + other_ref[b].astype(f32)
            first, second = [part[i] for part in parts]
            columns = [strip[:, 128 * c : 128 * c + 128] + (first[c] + second[c]) for c in range(4)]
            for column in columns:
                square = column * column
                total += square[:8] + square[8:]
            coded_ref[b] = encode(jnp.concatenate(columns, axis=1))
    square_ref[...] = jnp.broadcast_to(jnp.sum(total, keepdims=True), total.shape)
    fetch.wait()
    copies = []
    for p in range(coded_ref.shape[0] // 2):
        store(packed_ref, p, coded_ref[order_ref[2 * p]], coded_ref[order_ref[2 * p + 1]])
        if p % 4 == 3:
            rows = pl.ds(2 * ROWS * (p - 3), 8 * ROWS)
            copies.append(pltpu.make_async_copy(packed_ref.at[rows], out_ref.at[rows], sent.at[p // 4]))
            copies[-1].start()
    for copy in copies:
        copy.wait()


def owner_kernel(coded_ref, left_in, right_in, total_ref, left_out, right_out, out_ref, *scratch):
    grad_ref, left_ref, right_ref, done = scratch
    order = grad_ref.shape[0]
    reads = [pltpu.make_async_copy(a, b, done.at[i]) for i, (a, b) in enumerate([(left_in, left_ref), (right_in, right_ref)])]
    for copy in reads:
        copy.start()
    square = jnp.zeros((16, 128), f32)
    for p in range(order // 32):
        for i, coded in enumerate(load(coded_ref, p)):
            row = 16 * (2 * p + i)
            for c, piece in enumerate(decode(coded)):
                square += piece * piece
                grad_ref[row : row + 16, 128 * c : 128 * c + 128] = piece
    grad = split(grad_ref[...])
    for copy in reads:
        copy.wait()
    left_ref[...] = 0.95 * left_ref[...] + symmetric(grad, grad, ((1,), (1,))) * (1.0 / order)
    right_ref[...] = 0.95 * right_ref[...] + symmetric(grad, grad, ((0,), (0,))) * (1.0 / order)
    writes = [pltpu.make_async_copy(a, b, done.at[i]) for i, (a, b) in enumerate([(left_ref, left_out), (right_ref, right_out)])]
    for copy in writes:
        copy.start()
    half = dot3(split(inverse_root(left_ref[...])), grad)
    shaped = dot3(split(half), split(inverse_root(right_ref[...])))
    cells = 1.0 / (order * order)
    mean = jnp.sum(shaped * shaped, keepdims=True) * cells
    graft = jnp.sqrt(jnp.sum(square, keepdims=True) * cells + EPS) / jnp.sqrt(mean + EPS)
    grad_ref[...] = shaped
    number = encode_number(total_ref[...])
    for p in range(order // 32):
        rows = 32 * p
        store(
            out_ref,
            p,
            encode(grad_ref[rows : rows + 16, :], number, graft),
            encode(grad_ref[rows + 16 : rows + 32, :], number, graft),
        )
    for copy in writes:
        copy.wait()


def add_kernel(first_ref, second_ref, out_ref):
    out_ref[...] = first_ref[...] + second_ref[...]


def update_kernel(cells, owned_ref, coded_ref, out_ref, order_ref, wide_ref, done, fetched):
    fetch = pltpu.make_async_copy(owned_ref.at[lax.axis_index("dp")], order_ref, fetched)
    fetch.start()
    total = jnp.zeros((1, 128), f32)
    for p in range(wide_ref.shape[0] // 2):
        base = 2 * ROWS * p
        first = coded_ref[base + 64 : base + 80, :].astype(jnp.int32).astype(f32)[:8]
        second = coded_ref[base + 128 : base + 144, :].astype(jnp.int32).astype(f32)[8:]
        total += decode_number(first) + decode_number(second)
    layer = 1.0 / jnp.sqrt(total * (1.0 / cells) + EPS)
    fetch.wait()
    copies = []
    for p in range(wide_ref.shape[0] // 2):
        for i, coded in enumerate(load(coded_ref, p)):
            j = 2 * p + i
            for c, piece in enumerate(decode(coded, layer)):
                wide_ref[j, :, 128 * c : 128 * c + 128] = piece
            copies.append(pltpu.make_async_copy(wide_ref.at[j], out_ref.at[order_ref[j]], done.at[j]))
            copies[-1].start()
    for copy in copies:
        copy.wait()


def body(grads, owned, left_stat, right_stat):
    shards, groups = lax.axis_size("shard"), lax.axis_size("dp")
    blocks, strip, width = grads.shape[1:]
    chips = groups // 2
    square = jax.ShapeDtypeStruct((width, width), f32)
    wire = jax.ShapeDtypeStruct((shards * ROWS, 128), jnp.int16)
    grouped = grads[0].reshape(groups, shards, strip, width)
    swap = [(d, d ^ 1) for d in range(groups)]
    half_wire = pltpu.VMEM((shards // 8 * QUAD, 128), jnp.int16)
    number = jax.ShapeDtypeStruct((8, 128), f32)

    def cut(mebibytes, source, *wanted):
        return pl.pallas_call(
            lambda *refs: cut_kernel([(ahead % chips, other) for ahead, other in wanted], *refs),
            in_specs=[ANY],
            out_specs=[VMEM] * len(wanted),
            out_shape=[pltpu.VMEM((shards, strip, width), bf16)] * len(wanted),
            scratch_shapes=[pltpu.SemaphoreType.DMA((len(wanted),))],
            compiler_params=params(mebibytes),
            name=f"cut_{len(wanted)}",
        )(source)

    def partner(array):
        return lax.ppermute(array, "dp", swap)

    def along(ahead, array):
        return lax.ppermute(array, "dp", [(d, (d + 2 * ahead) % groups) for d in range(groups)])

    def pair_sum(half, own, other, *parts):
        return pl.pallas_call(
            lambda *refs: pair_kernel(half * shards // 2, *refs),
            in_specs=[VMEM] * (2 + len(parts)),
            out_specs=VMEM,
            out_shape=half_wire,
            compiler_params=params(4),
            name=f"pair_{half}_{len(parts)}",
        )(own, other, *parts)

    held, far = lax.optimization_barrier((grouped, cut(60, grouped, (2, 1))))
    far = partner(*far)
    own, *others = cut(57, held, (2, 0), (1, 1), (-1, 1))
    others = [partner(array) for array in others]
    left_relay, right_relay = pair_sum(0, own, far), pair_sum(1, own, far)
    held, left_relay, right_relay = lax.optimization_barrier((held, left_relay, right_relay))
    left_relay, right_relay = along(1, left_relay), along(-1, right_relay)
    *owns, other = cut(57, held, (1, 0), (-1, 0), (0, 0), (0, 1))
    ahead, behind, here = zip(owns, [*others, partner(other)])
    left_direct, right_direct = pair_sum(1, *ahead), pair_sum(0, *behind)
    right_direct = along(-1, right_direct)
    left_summed, right_summed = pair_sum(0, *ahead, left_relay), pair_sum(1, *behind, right_relay)
    left_summed, right_summed, left_direct = lax.optimization_barrier((left_summed, right_summed, left_direct))
    left_summed, right_summed = along(1, left_summed), along(-1, right_summed)
    left_direct = along(1, left_direct)
    strips, total = pl.pallas_call(
        sum_kernel,
        in_specs=[ANY] + [VMEM] * 6,
        out_specs=[ANY, VMEM],
        scratch_shapes=[
            pltpu.SMEM((shards,), jnp.int32),
            pltpu.VMEM((shards, ROWS, 128), jnp.int32),
            pltpu.VMEM(wire.shape, wire.dtype),
            pltpu.SemaphoreType.DMA,
            pltpu.SemaphoreType.DMA((shards // 8,)),
        ],
        out_shape=[wire, number],
        compiler_params=params(8),
        name="sum_strips",
    )(owned, *here, left_summed, right_direct, left_direct, right_summed)
    strips = lax.all_to_all(strips, "shard", split_axis=0, concat_axis=0, tiled=True)
    for bit in (1, 2, 4):
        other = lax.ppermute(total, "dp", [(d, d ^ bit) for d in range(groups)])
        total = pl.pallas_call(
            add_kernel,
            in_specs=[VMEM] * 2,
            out_specs=VMEM,
            out_shape=number,
            compiler_params=params(1),
            name=f"add_{bit}",
        )(total, other)
    left_fresh, right_fresh, pieces = pl.pallas_call(
        owner_kernel,
        in_specs=[VMEM, ANY, ANY, VMEM],
        out_specs=[ANY, ANY, VMEM],
        out_shape=[square, square, wire],
        scratch_shapes=[pltpu.VMEM((width, width), f32)] * 3 + [pltpu.SemaphoreType.DMA((2,))],
        compiler_params=params(24),
        name="owner",
    )(strips, left_stat[0, 0], right_stat[0, 0], total)
    pieces = lax.all_to_all(pieces, "shard", split_axis=0, concat_axis=0, tiled=True)
    update = pl.pallas_call(
        lambda *refs: update_kernel(blocks * width * width, *refs),
        in_specs=[ANY, VMEM],
        out_specs=ANY,
        out_shape=jax.ShapeDtypeStruct((shards, strip, width), f32),
        scratch_shapes=[
            pltpu.SMEM((shards,), jnp.int32),
            pltpu.VMEM((shards, strip, width), f32),
            pltpu.SemaphoreType.DMA((shards,)),
            pltpu.SemaphoreType.DMA,
        ],
        compiler_params=params(8),
        name="update",
    )(owned, pieces)
    return update, left_fresh[None, None], right_fresh[None, None]


def solution(mesh):
    return jax.shard_map(
        body,
        mesh=mesh,
        in_specs=(
            P("dp", None, "shard", None),
            P(),
            P("dp", "shard", None, None),
            P("dp", "shard", None, None),
        ),
        out_specs=(
            P("dp", "shard", None),
            P("dp", "shard", None, None),
            P("dp", "shard", None, None),
        ),
        check_vma=False,
    )
```
